256 devices in a mesh: beam: 128 (over x_hi, y, z, core), tm: 2 (over x_lo).
Axes of the slice: x: 4 (x_hi: 2, x_lo: 2; x = x_hi * 2 + x_lo), y: 4, z: 8, core: 2. Of those that a mesh axis runs over, the one named last changes fastest.
Arguments:
- voltages: bfloat16 [2, 16, 8192, 2048], P(None, 'tm', 'beam'), may hold values from -6 to 6
- feed_slot: int32 [2048], replicated, may hold values from 0 to 2047, each once
- tree_shift: int32 [14], replicated, may hold values from 0 to 4, as said below
Outputs:
- search: float32 [1024, 2, 16, 512], P('beam', None, 'tm')
The draws below stay inside these ranges and needn't reach their ends.
Inputs may be any that keep to these rules, and one draw needn't show every extreme that they name: `feed_slot`: every grid slot holds exactly one feed. `tree_shift`: the entries 2^(s+1) - 2 to 2^(s+2) - 3 are the lags of section s for trials k = 0 .. 2^(s+1) - 1; each lies between 0 and 2^s, and the last trial of every section has lag exactly 2^s.
All inputs are finite; a program needn't handle non-finite values.
Results may differ from the reference program's by a relative error of at most 0.00083.
Values sent between devices are 32-bit elements; how exact they have to be, the bound alone decides.
A program may use at most 128 MiB of HBM per device.

```python
import math
import jax
import jax.numpy as jnp
from jax import lax

POL = 2
EW = 4
NS = 256
FEEDS = 2048
BEAMS = 1024
CHANNELS = 8192
FSUM = 16
NCH = 512
LEVELS = 3
BOXES = 2
TIME = 16


def draw_tree_shift(key, part):
    key = jax.random.fold_in(key, 7)
    pieces = []
    for level_index in range(LEVELS):
        trials = 2 ** (level_index + 1)
        max_lag = 2 ** level_index
        classic = (jnp.arange(trials, dtype=jnp.int32) + 1) // 2
        jitter = jax.random.randint(jax.random.fold_in(key, level_index), (trials,), -1, 2, dtype=jnp.int32)
        lagged = jnp.clip(classic + jitter, 0, max_lag)
        lagged = lagged.at[trials - 1].set(max_lag)
        pieces.append(lagged)
    return jnp.concatenate(pieces).astype(jnp.int32)


def shard_levels(own_key, shape, split, low, high):
    level = 1.0
    for dim, shards_of in split:
        heights = jax.random.uniform(jax.random.fold_in(jax.random.fold_in(own_key, 6), dim), (shards_of,), jnp.float32, low / len(split), high / len(split))
        level = level * jnp.repeat(jnp.exp(heights), shape[dim] // shards_of).reshape((-1,) + (1,) * (len(shape) - 1 - dim))
    return level


def gaussian(key, extent, spread, reach, shards=(), held_as=jnp.bfloat16):
    array = jax.random.normal(key, extent, jnp.float32) * spread
    if len(shards) > 0:
        array = shard_levels(key, extent, shards, -0.22, 0.18) * array
    return jnp.clip(array, min=-reach, max=reach).astype(held_as)


def setup_inputs(seed: int = 0) -> dict:
    splits = jax.random.split(jax.random.key(seed), 4)
    voltages = gaussian(splits[0], (2, TIME, CHANNELS, FEEDS), 1.0, 6.0, ((1, 2), (2, 128)))
    feed_slot = jax.random.permutation(splits[1], FEEDS).astype(jnp.int32)
    tree_shift = draw_tree_shift(jax.random.fold_in(splits[3], 71), 0)
    return dict(voltages=voltages, feed_slot=feed_slot, tree_shift=tree_shift)


def dft_tables(length):
    index = jnp.arange(length, dtype=jnp.int32)
    phase = (index[:, None] * index[None, :]) % length
    angle = phase.astype(jnp.float32) * (2.0 * math.pi / length)
    return jnp.cos(angle).astype(jnp.bfloat16), jnp.sin(angle).astype(jnp.bfloat16)


def quarter_turn(real_part, imag_part, turns):
    if turns == 0:
        return real_part, imag_part
    if turns == 1:
        return imag_part, -real_part
    if turns == 2:
        return -real_part, -imag_part
    return -imag_part, real_part


def east_west(north_real, north_imag, factor):
    columns = []
    for column in range(EW):
        sum_real = None
        sum_imag = None
        for cylinder in range(EW):
            turned_real, turned_imag = quarter_turn(north_real[:, :, cylinder, :], north_imag[:, :, cylinder, :], (column * cylinder) % 4)
            if sum_real is None:
                sum_real, sum_imag = turned_real, turned_imag
            else:
                sum_real = sum_real + turned_real
                sum_imag = sum_imag + turned_imag
        energy = sum_real * sum_real + sum_imag * sum_imag
        columns.append((energy[:, 0, :] + energy[:, 1, :]) * factor)
    return jnp.concatenate(columns, axis=1)


def frame_bins(frame_volts, slot_owner, cos_wide, sin_wide):
    gridded = jnp.take(frame_volts, slot_owner, axis=2)
    real_part = gridded[0].reshape(-1, NS).astype(jnp.float32)
    imag_part = gridded[1].reshape(-1, NS).astype(jnp.float32)
    highest = lax.Precision.HIGHEST
    north_real = jnp.dot(real_part, cos_wide, precision=highest, preferred_element_type=jnp.float32) + jnp.dot(imag_part, sin_wide, precision=highest, preferred_element_type=jnp.float32)
    north_imag = jnp.dot(imag_part, cos_wide, precision=highest, preferred_element_type=jnp.float32) - jnp.dot(real_part, sin_wide, precision=highest, preferred_element_type=jnp.float32)
    beam_power = east_west(north_real.reshape(-1, POL, EW, NS), north_imag.reshape(-1, POL, EW, NS), 0.5 / FEEDS)
    binned = jnp.sum(beam_power.reshape(NCH, FSUM, BEAMS), axis=1)
    return jnp.transpose(binned, (1, 0))


def tree_step(current, shifts, level_index):
    max_lag = 2 ** level_index
    frame_count, beam_count, band_total = current.shape
    grouped = current.reshape(frame_count, beam_count, band_total // (2 * max_lag), 2, max_lag)
    lower_band = grouped[:, :, :, 0, :]
    upper_band = grouped[:, :, :, 1, :]
    tail = jnp.zeros((max_lag,) + upper_band.shape[1:], upper_band.dtype)
    extended = jnp.concatenate([upper_band, tail], axis=0)
    lower_twice = jnp.repeat(lower_band, 2, axis=-1)
    upper_twice = jnp.repeat(extended, 2, axis=-1)
    shifted = jnp.zeros_like(lower_twice)
    for offset in range(max_lag + 1):
        shifted = shifted + jnp.where(shifts == offset, upper_twice[offset:offset + frame_count], 0.0)
    return (lower_twice + shifted).reshape(frame_count, beam_count, band_total)


def boxcar_sums(series, frames):
    widest = 2 ** (BOXES - 1)
    running = series[:frames + widest - 1]
    results = []
    for box_index in range(BOXES):
        if box_index > 0:
            half_span = 2 ** (box_index - 1)
            running = running[:-half_span] + running[half_span:]
        results.append(running[:frames] * (1.0 / (FSUM * 2 ** LEVELS * 2 ** box_index)))
    return jnp.transpose(jnp.stack(results, axis=1), (2, 1, 0, 3))


def reference(voltages, feed_slot, tree_shift):
    slot_owner = jnp.zeros((FEEDS,), jnp.int32).at[feed_slot].set(jnp.arange(FEEDS, dtype=jnp.int32))
    cos_table, sin_table = dft_tables(NS)
    cos_wide = cos_table.astype(jnp.float32)
    sin_wide = sin_table.astype(jnp.float32)

    def one_frame(frame_index):
        frame_volts = lax.dynamic_index_in_dim(voltages, frame_index, 1, keepdims=False)
        return frame_bins(frame_volts, slot_owner, cos_wide, sin_wide)

    current = lax.map(one_frame, jnp.arange(TIME, dtype=jnp.int32))
    for level_index in range(LEVELS):
        shifts = tree_shift[2 ** (level_index + 1) - 2:2 ** (level_index + 2) - 2]
        current = tree_step(current, shifts, level_index)
    widest = 2 ** (BOXES - 1)
    padding = jnp.zeros((widest - 1,) + current.shape[1:], current.dtype)
    series = jnp.concatenate([current, padding], axis=0)
    return boxcar_sums(series, TIME)
```

```python
import math

import jax
import jax.numpy as jnp
import numpy as np
from jax import lax
from jax.experimental import pallas as pl
from jax.experimental.pallas import tpu as pltpu
from jax.sharding import PartitionSpec as P

POL = 2
EW = 4
NS = 256
FEEDS = 2048
FSUM = 16
LEVELS = 3
BOXES = 2
FRAMES = 8
CHANS = 64
SAMPLES = FRAMES * CHANS
BANDS = CHANS // FSUM
LANES = 128
MESH = pl.DeviceIdType.MESH


def steer_table():
    index = np.arange(NS)
    phase = (index[:, None] * index[None, :]) % NS
    angle = phase.astype(np.float32) * np.float32(2.0 * math.pi / NS)
    order = [high * 16 + core * 8 + low for core in range(2) for high in range(16) for low in range(8)]
    cos_table = np.cos(angle).astype(np.float32)[order]
    sin_table = np.sin(angle).astype(np.float32)[order]
    top = np.concatenate([cos_table, sin_table], axis=1)
    bottom = np.concatenate([-sin_table, cos_table], axis=1)
    return jnp.asarray(np.concatenate([top, bottom], axis=0), jnp.bfloat16)


def bin_table():
    table = np.zeros((BANDS * FRAMES, SAMPLES), np.float32)
    for frame in range(FRAMES):
        for chan in range(CHANS):
            table[(chan // FSUM) * FRAMES + frame, frame * CHANS + chan] = 0.5 / FEEDS
    return jnp.asarray(table, jnp.bfloat16)


def beams_kernel(slot_ref, volt_ref, steer_ref, bin_ref, eye_ref, out_ref, turned, gridded, north, power):
    contract_last = (((1,), (1,)), ((), ()))
    for part in range(4):
        rows = volt_ref[pl.ds(part * 256, 256), :]
        for block in range(8):
            flipped = lax.dot_general(
                eye_ref[...], rows[:, block * 256 : block * 256 + 256], contract_last,
                preferred_element_type=jnp.float32,
            )
            for half in range(2):
                turned[pl.ds(block * 2048 + part * 2 + half, 256, stride=8), :] = flipped[
                    :, half * LANES : half * LANES + LANES
                ]

    def move(feed, carry):
        slot = slot_ref[feed]
        gridded[pl.ds(pl.multiple_of(slot * 8, 8), 8), :] = turned[pl.ds(pl.multiple_of(feed * 8, 8), 8), :]
        return carry

    lax.fori_loop(0, FEEDS, move, 0, unroll=16)

    for pol in range(POL):
        for cyl in range(EW):
            first = (pol * EW + cyl) * NS * 8
            parts = [gridded[pl.ds(first + q, NS, stride=8), :].astype(jnp.bfloat16) for q in range(8)]
            both = jnp.concatenate(
                [jnp.concatenate(parts[:4], axis=1), jnp.concatenate(parts[4:], axis=1)], axis=0
            )
            north[cyl] = jnp.dot(steer_ref[...], both, preferred_element_type=jnp.float32)
        for strip in range(16):
            top = pl.ds(strip * 16, 16)
            low = pl.ds(NS + strip * 16, 16)
            re = [north[cyl, top, :] for cyl in range(EW)]
            im = [north[cyl, low, :] for cyl in range(EW)]
            even_re, even_im = re[0] + re[2], im[0] + im[2]
            odd_re, odd_im = re[0] - re[2], im[0] - im[2]
            side_re, side_im = re[1] + re[3], im[1] + im[3]
            diff_re, diff_im = re[1] - re[3], im[1] - im[3]
            sums = [
                (even_re + side_re, even_im + side_im),
                (odd_re + diff_im, odd_im - diff_re),
                (even_re - side_re, even_im - side_im),
                (odd_re - diff_im, odd_im + diff_re),
            ]
            for column in range(EW):
                energy = sums[column][0] * sums[column][0] + sums[column][1] * sums[column][1]
                if pol == 0:
                    power[column, top, :] = energy
                else:
                    power[column, top, :] += energy
    for column in range(EW):
        whole = power[column]
        high = whole.astype(jnp.bfloat16)
        rest = (whole - high.astype(jnp.float32)).astype(jnp.bfloat16)
        binned = lax.dot_general(
            bin_ref[...], high, contract_last, preferred_element_type=jnp.float32
        ) + lax.dot_general(bin_ref[...], rest, contract_last, preferred_element_type=jnp.float32)
        for core in range(2):
            out_ref[core * 2 + column // 2, column % 2] = binned[:, core * LANES : core * LANES + LANES]


def beams(voltages, feed_slot):
    return pl.pallas_call(
        beams_kernel,
        out_shape=jax.ShapeDtypeStruct((4, 2, BANDS * FRAMES, LANES), jnp.float32),
        in_specs=[pl.BlockSpec(memory_space=pltpu.SMEM)] + [pl.BlockSpec(memory_space=pltpu.VMEM)] * 4,
        out_specs=pl.BlockSpec(memory_space=pltpu.VMEM),
        scratch_shapes=[
            pltpu.VMEM((FEEDS * 8, LANES), jnp.float32),
            pltpu.VMEM((FEEDS * 8, LANES), jnp.float32),
            pltpu.VMEM((EW, 2 * NS, SAMPLES), jnp.float32),
            pltpu.VMEM((EW, NS, SAMPLES), jnp.float32),
        ],
        compiler_params=pltpu.CompilerParams(vmem_limit_bytes=48 * 2**20),
        name="beams",
    )(
        feed_slot,
        voltages.reshape(2 * SAMPLES, FEEDS),
        steer_table(),
        bin_table(),
        jnp.asarray(np.eye(256), jnp.bfloat16),
    )


def swap_chunks(tiles):
    lane = lax.broadcasted_iota(jnp.int32, (8, LANES), 1)
    tiles = list(tiles)
    for bit in range(4):
        span = 8 << bit
        low_half = (lane // span) % 2 == 0
        for first in range(16):
            if first >> bit & 1:
                continue
            second = first | 1 << bit
            one, two = tiles[first], tiles[second]
            tiles[first] = jnp.where(low_half, one, pltpu.roll(two, span, 1))
            tiles[second] = jnp.where(low_half, pltpu.roll(one, LANES - span, 1), two)
    return tiles


def search_kernel(
    shift_ref, own_ref, out_ref, level_0, level_1, level_2, series, packed, landed, result,
    near_send, near_recv, far_send, far_recv, self_sem, out_sem,
):
    place = lax.axis_index("beam")
    half = lax.axis_index("tm")
    core = lax.rem(place, 2)
    site = lax.div(place, 2)
    sites = lax.axis_size("beam") // 2
    side = lax.div(site, 32)
    own_slot = side == half

    landed[:, 4:8, :] = jnp.zeros((sites, 4, LANES), jnp.float32)
    barrier = pltpu.get_barrier_semaphore()

    def peer(c, h):
        return (site * 2 + c, h)

    for other in range(1, 4):
        c = lax.rem(core + other // 2, 2)
        h = lax.rem(half + other % 2, 2)
        pl.semaphore_signal(barrier, inc=1, device_id=peer(c, h), device_id_type=MESH)

    def greet(step, carry):
        from_site = lax.rem(site + step, sites)

        @pl.when(jnp.logical_not(jnp.logical_and(from_site == site, own_slot)))
        def _():
            pl.semaphore_signal(barrier, inc=1, device_id=(from_site * 2 + core, side), device_id_type=MESH)

        return carry

    lax.fori_loop(0, sites, greet, 0)
    pl.semaphore_wait(barrier, jnp.where(own_slot, sites + 2, sites + 3))

    here = (
        slice(None),
        pl.ds(core * BANDS, BANDS),
        pl.ds(pl.multiple_of(half * FRAMES, FRAMES), FRAMES),
        slice(None),
    )
    copies = []
    for other in range(1, 4):
        c = lax.rem(core + other // 2, 2)
        h = lax.rem(half + other % 2, 2)
        copy = pltpu.make_async_remote_copy(
            src_ref=own_ref.at[c * 2 + h],
            dst_ref=level_0.at[here],
            send_sem=near_send.at[other],
            recv_sem=near_recv.at[other],
            device_id=peer(c, h),
            device_id_type=MESH,
        )
        copy.start()
        copies.append(copy)
    mine = pltpu.make_async_copy(own_ref.at[core * 2 + half], level_0.at[here], self_sem)
    mine.start()
    for buffer in (level_0, level_1, level_2):
        buffer[:, :, 16:24, :] = jnp.zeros((2, 8, 8, LANES), jnp.float32)
    mine.wait()
    for copy in copies:
        copy.wait()

    buffers = (level_0, level_1, level_2)
    for level in range(LEVELS):
        span = 2**level
        current = buffers[level]
        for band in range(8):
            base, k = band - band % (2 * span), band % (2 * span)
            lower = base + k // 2
            lag = shift_ref[2 * span - 2 + k]
            for column in range(2):
                total = (
                    current[column, lower, 0:16, :] + current[column, lower + span, pl.ds(lag, 16), :]
                )
                if level < LEVELS - 1:
                    buffers[level + 1][column, band, 0:16, :] = total
                else:
                    series[column, pl.ds(band, 16, stride=8), :] = total
    lane = lax.broadcasted_iota(jnp.int32, (8, LANES), 1)
    row = lax.broadcasted_iota(jnp.int32, (8, LANES), 0)
    keep = (lane < LANES // 2) == (row < 4)
    for column in range(2):
        flipped = jnp.transpose(series[column])
        for target in range(16):
            tile = flipped[target * 8 : target * 8 + 8]
            crossed = pltpu.roll(pltpu.roll(tile, 4, 0), LANES // 2, 1)
            packed[column * 16 + target] = jnp.where(keep, tile, crossed)

    def to_early(target):
        return pltpu.make_async_remote_copy(
            src_ref=packed.at[target],
            dst_ref=landed.at[site],
            send_sem=far_send.at[0],
            recv_sem=far_recv,
            device_id=((half * 32 + target) * 2 + core, 0),
            device_id_type=MESH,
        )

    def to_late(target):
        return pltpu.make_async_remote_copy(
            src_ref=packed.at[target, 4:8],
            dst_ref=landed.at[site, 0:4],
            send_sem=far_send.at[1],
            recv_sem=far_recv,
            device_id=((half * 32 + target) * 2 + core, 1),
            device_id_type=MESH,
        )

    def send(step, carry):
        target = lax.rem(site + step, 32)
        is_self = half * 32 + target == site

        @pl.when(jnp.logical_not(jnp.logical_and(is_self, half == 0)))
        def _():
            to_early(target).start()

        @pl.when(jnp.logical_not(jnp.logical_and(is_self, half == 1)))
        def _():
            to_late(target).start()

        return carry

    lax.fori_loop(0, 32, send, 0)
    own_target = lax.rem(site, 32)

    @pl.when(jnp.logical_and(own_slot, half == 0))
    def _():
        copy = pltpu.make_async_copy(packed.at[own_target], landed.at[site], self_sem)
        copy.start()
        copy.wait()

    @pl.when(jnp.logical_and(own_slot, half == 1))
    def _():
        copy = pltpu.make_async_copy(packed.at[own_target, 4:8], landed.at[site, 0:4], self_sem)
        copy.start()
        copy.wait()

    def wait_recv(count, rows):
        pltpu.make_async_copy(landed.at[0:count, 0:rows], landed.at[0:count, 0:rows], far_recv).wait()

    @pl.when(half == 0)
    def _():
        @pl.when(own_slot)
        def _():
            wait_recv(sites - 1, 8)

        @pl.when(jnp.logical_not(own_slot))
        def _():
            wait_recv(sites, 8)

    @pl.when(half == 1)
    def _():
        @pl.when(own_slot)
        def _():
            wait_recv(sites - 1, 4)

        @pl.when(jnp.logical_not(own_slot))
        def _():
            wait_recv(sites, 4)

    writes = []
    for block in range(4):
        tiles = swap_chunks([landed[block * 16 + g] for g in range(16)])
        for high in range(2):
            for frame in range(8):
                now = tiles[high * 8 + frame]
                if frame < 7:
                    later = tiles[high * 8 + frame + 1]
                else:
                    later = pltpu.roll(tiles[high * 8], 4, 0)
                first = high * 64 + frame
                result[block, pl.ds(first, 4, stride=16), :] = (now * (1.0 / (FSUM * 8)))[0:4]
                result[block, pl.ds(first + 8, 4, stride=16), :] = ((now + later) * (1.0 / (FSUM * 16)))[0:4]

        write = pltpu.make_async_copy(result.at[block], out_ref.at[:, pl.ds(block * LANES, LANES)], out_sem.at[block])
        write.start()
        writes.append(write)

    def wait_send(index, count, rows):
        pltpu.make_async_copy(packed.at[0:count, 0:rows], packed.at[0:count, 0:rows], far_send.at[index]).wait()

    early_self = jnp.logical_and(own_slot, half == 0)
    late_self = jnp.logical_and(own_slot, half == 1)
    for flag, index, rows in ((early_self, 0, 8), (late_self, 1, 4)):
        @pl.when(flag)
        def _():
            wait_send(index, 31, rows)

        @pl.when(jnp.logical_not(flag))
        def _():
            wait_send(index, 32, rows)

    for write in writes:
        write.wait()


def search(binned, tree_shift):
    level = pltpu.VMEM((2, 8, 24, LANES), jnp.float32)
    return pl.pallas_call(
        search_kernel,
        out_shape=jax.ShapeDtypeStruct((8 * BOXES * FRAMES, 512), jnp.float32),
        in_specs=[pl.BlockSpec(memory_space=pltpu.SMEM), pl.BlockSpec(memory_space=pltpu.VMEM)],
        out_specs=pl.BlockSpec(memory_space=pl.ANY),
        scratch_shapes=[
            level,
            level,
            level,
            pltpu.VMEM((2, 128, LANES), jnp.float32),
            pltpu.VMEM((32, 8, LANES), jnp.float32),
            pltpu.VMEM((64, 8, LANES), jnp.float32),
            pltpu.VMEM((4, 128, LANES), jnp.float32),
            pltpu.SemaphoreType.DMA((4,)),
            pltpu.SemaphoreType.DMA((4,)),
            pltpu.SemaphoreType.DMA((2,)),
            pltpu.SemaphoreType.DMA,
            pltpu.SemaphoreType.DMA,
            pltpu.SemaphoreType.DMA((4,)),
        ],
        compiler_params=pltpu.CompilerParams(
            collective_id=0, has_side_effects=True, vmem_limit_bytes=16 * 2**20
        ),
        name="search",
    )(tree_shift, binned.reshape(4, 2, BANDS, FRAMES, LANES))


def on_device(voltages, feed_slot, tree_shift):
    binned = beams(voltages, feed_slot)
    result = search(binned, tree_shift)
    return result.reshape(8, BOXES, FRAMES, 512)


def solution(mesh):
    placed = (P(None, "tm", "beam", None), P(), P())
    return jax.shard_map(
        on_device,
        mesh=mesh,
        in_specs=placed,
        out_specs=P("beam", None, "tm", None),
        check_vma=False,
    )
```

```python
import math

import jax
import jax.numpy as jnp
import ml_dtypes
import numpy as np
from jax import lax
from jax.experimental import pallas as pl
from jax.experimental.pallas import tpu as pltpu
from jax.sharding import PartitionSpec as P

POL = 2
EW = 4
NS = 256
FEEDS = 2048
FSUM = 16
LEVELS = 3
BOXES = 2
FRAMES = 8
CHANS = 64
SAMPLES = FRAMES * CHANS
BANDS = CHANS // FSUM
MEMBERS = 16
LANES = 128
MESH = pl.DeviceIdType.MESH


def steer_tables():
    index = np.arange(NS)
    phase = (index[:, None] * index[None, :]) % NS
    angle = phase.astype(np.float32) * np.float32(2.0 * math.pi / NS)
    order = [high * 16 + core * 8 + low for core in range(2) for high in range(16) for low in range(8)]
    both = np.concatenate([np.cos(angle)[order], np.sin(angle)[order]], axis=1)
    return jnp.asarray(both.astype(ml_dtypes.bfloat16).astype(np.float32))


def contract_last(left, right):
    return lax.dot_general(left, right, (((1,), (1,)), ((), ())), preferred_element_type=jnp.float32)


def iota(shape, dim):
    return lax.broadcasted_iota(jnp.int32, shape, dim)


def swap_chunks(tiles):
    lane = lax.broadcasted_iota(jnp.int32, (8, LANES), 1)
    tiles = list(tiles)
    for bit in range(4):
        span = 8 << bit
        low_half = (lane // span) % 2 == 0
        for first in range(16):
            if first >> bit & 1:
                continue
            second = first | 1 << bit
            one, two = tiles[first], tiles[second]
            tiles[first] = jnp.where(low_half, one, pltpu.roll(two, span, 1))
            tiles[second] = jnp.where(low_half, pltpu.roll(one, LANES - span, 1), two)
    return tiles


def search_kernel(
    slot_hbm, shift_hbm, volt_hbm, tables_hbm, out_ref,
    slot, owner_vmem, owner, shift_ref, volts, tables, turned, gridded, north,
    own_ref, near, level_0, level_1, level_2, series, packed, landed, result,
    slot_sem, owner_sem, shift_sem, volt_sem, steer_sem,
    near_send, near_recv, far_send, far_recv, self_sem, out_sem,
):
    slot_copy = pltpu.make_async_copy(slot_hbm, slot, slot_sem)
    steer_copy = pltpu.make_async_copy(tables_hbm, tables, steer_sem)
    shift_copy = pltpu.make_async_copy(shift_hbm, shift_ref, shift_sem)
    volt_copies = [
        pltpu.make_async_copy(volt_hbm.at[pl.ds(part * 256, 256)], volts.at[pl.ds(part * 256, 256)], volt_sem.at[part])
        for part in range(4)
    ]
    for copy in [slot_copy] + volt_copies + [steer_copy, shift_copy]:
        copy.start()

    landed[:, :, 4:8, :] = jnp.zeros((16, 4, 4, LANES), jnp.float32)
    for buffer in (level_0, level_1, level_2):
        buffer[:, :, 16:24, :] = jnp.zeros((2, 8, 8, LANES), jnp.float32)
    place = lax.axis_index("beam")
    half = lax.axis_index("tm")
    core = lax.rem(place, 2)
    site = lax.div(place, 2)
    z = lax.rem(site, 8)
    y = lax.rem(lax.div(site, 8), 4)
    x_high = lax.div(site, 32)
    member = (core * 2 + half) * 4 + y
    selfish = x_high == half

    def of_member(other):
        c, h, at = lax.div(other, 8), lax.rem(lax.div(other, 4), 2), lax.rem(other, 4)
        return (((x_high * 4 + at) * 8 + z) * 2 + c, h)

    def at_site(xx, zz, h):
        return (((xx * 4 + y) * 8 + zz) * 2 + core, h)

    barrier = pltpu.get_barrier_semaphore()

    def greet(step, carry):
        pl.semaphore_signal(
            barrier, inc=1, device_id=of_member(lax.rem(member + step, MEMBERS)), device_id_type=MESH
        )
        return carry

    lax.fori_loop(1, MEMBERS, greet, 0)

    def greet_far(step, carry):
        xx, zz = lax.div(step, 8), lax.rem(z + step, 8)

        @pl.when(jnp.logical_not(jnp.logical_and(jnp.logical_and(xx == x_high, zz == z), selfish)))
        def _():
            pl.semaphore_signal(barrier, inc=1, device_id=at_site(xx, zz, x_high), device_id_type=MESH)

        return carry

    lax.fori_loop(0, 16, greet_far, 0)
    slot_copy.wait()
    places = iota((FEEDS // LANES, LANES), 0) * LANES + iota((FEEDS // LANES, LANES), 1)
    found = [jnp.zeros((FEEDS // LANES, LANES), jnp.int32) for _ in range(4)]
    for part in range(4):
        volt_copies[part].wait()
        rows = volts[pl.ds(part * 256, 256), :]
        for block in range(8):
            flipped = jnp.transpose(rows[:, block * 256 : block * 256 + 256]).astype(jnp.float32)
            for half_rows in range(2):
                turned[pl.ds(block * 2048 + part * 2 + half_rows, 256, stride=8), :] = flipped[
                    :, half_rows * LANES : half_rows * LANES + LANES
                ]
            if part < 2:
                row = part * 8 + block
                for lane in range(LANES):
                    found[lane % 4] = jnp.where(places == slot[row, lane], row * LANES + lane, found[lane % 4])
        if part == 1:
            owner_vmem[...] = jnp.maximum(jnp.maximum(found[0], found[1]), jnp.maximum(found[2], found[3]))
            owner_copy = pltpu.make_async_copy(owner_vmem, owner, owner_sem)
            owner_copy.start()

    owner_copy.wait()

    def move(row, carry):
        for lane in range(LANES):
            feed = owner[row, lane]
            first = pl.multiple_of((row * LANES + lane) * 8, 8)
            gridded[pl.ds(first, 8), :] = turned[pl.ds(feed * 8, 8), :]
        return carry

    lax.fori_loop(0, FEEDS // LANES, move, 0)

    steer_copy.wait()
    top = tables[...].astype(jnp.bfloat16)
    steer = jnp.concatenate([top, jnp.concatenate([-top[:, NS:], top[:, :NS]], axis=1)], axis=0)
    for pol in range(POL):
        for cyl in range(EW):
            first = (pol * EW + cyl) * NS * 8
            parts = [gridded[pl.ds(first + q, NS, stride=8), :].astype(jnp.bfloat16) for q in range(8)]
            both = jnp.concatenate(
                [jnp.concatenate(parts[:4], axis=1), jnp.concatenate(parts[4:], axis=1)], axis=0
            )
            north[pol * EW + cyl] = jnp.dot(steer, both, preferred_element_type=jnp.float32)

    bin_row, sample = iota((BANDS * FRAMES, SAMPLES), 0), iota((BANDS * FRAMES, SAMPLES), 1)
    chosen = (sample // CHANS == bin_row % FRAMES) & (sample % CHANS // FSUM == bin_row // FRAMES)
    adder = jnp.where(chosen, 0.5 / FEEDS, 0.0).astype(jnp.bfloat16)
    binned = [[] for _ in range(EW)]
    for strip in range(2):
        energies = [[] for _ in range(EW)]
        for piece in range(8):
            top = pl.ds(strip * 128 + piece * 16, 16)
            low = pl.ds(NS + strip * 128 + piece * 16, 16)
            power = [None] * EW
            for pol in range(POL):
                re = [north[pol * EW + cyl, top, :] for cyl in range(EW)]
                im = [north[pol * EW + cyl, low, :] for cyl in range(EW)]
                even_re, even_im = re[0] + re[2], im[0] + im[2]
                odd_re, odd_im = re[0] - re[2], im[0] - im[2]
                side_re, side_im = re[1] + re[3], im[1] + im[3]
                diff_re, diff_im = re[1] - re[3], im[1] - im[3]
                sums = [
                    (even_re + side_re, even_im + side_im),
                    (odd_re + diff_im, odd_im - diff_re),
                    (even_re - side_re, even_im - side_im),
                    (odd_re - diff_im, odd_im + diff_re),
                ]
                for column in range(EW):
                    energy = sums[column][0] * sums[column][0] + sums[column][1] * sums[column][1]
                    power[column] = energy if pol == 0 else power[column] + energy
            for column in range(EW):
                energies[column].append(power[column])
        for column in range(EW):
            whole = jnp.concatenate(energies[column], axis=0)
            high = whole.astype(jnp.bfloat16)
            rest = (whole - high.astype(jnp.float32)).astype(jnp.bfloat16)
            binned[column].append(contract_last(adder, high) + contract_last(adder, rest))
    low_lanes = iota((16, LANES), 1) < LANES // 2
    for column in range(EW):
        for c in range(2):
            one, two = binned[column][c][0:16], binned[column][c][16:32]
            target = (c * 2 + column // 2) * 4 + column % 2 * 2
            own_ref[target] = jnp.where(low_lanes, one, pltpu.roll(two, LANES // 2, 1))
            own_ref[target + 1] = jnp.where(low_lanes, pltpu.roll(one, LANES // 2, 1), two)


    pl.semaphore_wait(barrier, jnp.where(selfish, MEMBERS + 14, MEMBERS + 15))

    def near_copy(other):
        return pltpu.make_async_remote_copy(
            src_ref=own_ref.at[other],
            dst_ref=near.at[member],
            send_sem=near_send,
            recv_sem=near_recv,
            device_id=of_member(other),
            device_id_type=MESH,
        )

    def send_near(step, carry):
        near_copy(lax.rem(member + step, MEMBERS)).start()
        return carry

    lax.fori_loop(1, MEMBERS, send_near, 0)
    mine = pltpu.make_async_copy(own_ref.at[member], near.at[member], self_sem)
    mine.start()
    mine.wait()
    pltpu.make_async_copy(near.at[0:15], near.at[0:15], near_recv).wait()

    shift_copy.wait()
    low_frames = iota((FRAMES, LANES), 1) < LANES // 2
    for c in range(2):
        for h in range(2):
            for pair in range(2):
                first = (c * 2 + h) * 4 + pair * 2
                for low in range(2):
                    one, two = near[first, low * 8 : low * 8 + 8, :], near[first + 1, low * 8 : low * 8 + 8, :]
                    frames = slice(h * 8, h * 8 + 8)
                    level_0[pair, c * 4 + low, frames, :] = jnp.where(low_frames, one, pltpu.roll(two, LANES // 2, 1))
                    level_0[pair, c * 4 + 2 + low, frames, :] = jnp.where(
                        low_frames, pltpu.roll(one, LANES // 2, 1), two
                    )

    buffers = (level_0, level_1, level_2)
    for level in range(LEVELS):
        span = 2**level
        current = buffers[level]
        for band in range(8):
            base, k = band - band % (2 * span), band % (2 * span)
            lower = base + k // 2
            lag = shift_ref[2 * span - 2 + k]
            for pair in range(2):
                total = current[pair, lower, 0:16, :] + current[pair, lower + span, pl.ds(lag, 16), :]
                if level < LEVELS - 1:
                    buffers[level + 1][pair, band, 0:16, :] = total
                else:
                    series[pair, pl.ds(band, 16, stride=8), :] = total
    keep = (iota((8, LANES), 1) < LANES // 2) == (iota((8, LANES), 0) < 4)
    for pair in range(2):
        flipped = jnp.transpose(series[pair])
        for low in range(2):
            for target in range(8):
                first = low * 64 + target * 8
                tile = flipped[first : first + 8]
                crossed = pltpu.roll(pltpu.roll(tile, 4, 0), LANES // 2, 1)
                packed[target, pair * 2 + low] = jnp.where(keep, tile, crossed)

    slot = x_high * 8 + z

    def to_early(target):
        return pltpu.make_async_remote_copy(
            src_ref=packed.at[target],
            dst_ref=landed.at[slot],
            send_sem=far_send.at[0],
            recv_sem=far_recv,
            device_id=at_site(half, target, 0),
            device_id_type=MESH,
        )

    def to_late(target):
        return pltpu.make_async_remote_copy(
            src_ref=packed.at[target, :, 4:8],
            dst_ref=landed.at[slot, :, 0:4],
            send_sem=far_send.at[1],
            recv_sem=far_recv,
            device_id=at_site(half, target, 1),
            device_id_type=MESH,
        )

    early_self = jnp.logical_and(selfish, half == 0)
    late_self = jnp.logical_and(selfish, half == 1)

    def send(step, carry):
        target = lax.rem(z + step, 8)

        @pl.when(jnp.logical_not(jnp.logical_and(target == z, early_self)))
        def _():
            to_early(target).start()

        @pl.when(jnp.logical_not(jnp.logical_and(target == z, late_self)))
        def _():
            to_late(target).start()

        return carry

    lax.fori_loop(0, 8, send, 0)

    @pl.when(early_self)
    def _():
        copy = pltpu.make_async_copy(packed.at[z], landed.at[slot], self_sem)
        copy.start()
        copy.wait()

    @pl.when(late_self)
    def _():
        copy = pltpu.make_async_copy(packed.at[z, :, 4:8], landed.at[slot, :, 0:4], self_sem)
        copy.start()
        copy.wait()

    def wait_for(buffer, sem, count, rows):
        part = buffer.at[0:count, :, 0:rows]
        pltpu.make_async_copy(part, part, sem).wait()

    for h, rows in ((0, 8), (1, 4)):
        @pl.when(jnp.logical_and(half == h, selfish))
        def _():
            wait_for(landed, far_recv, 15, rows)

        @pl.when(jnp.logical_and(half == h, jnp.logical_not(selfish)))
        def _():
            wait_for(landed, far_recv, 16, rows)

    writes = []
    for block in range(4):
        xx, pair = block // 2, block % 2
        tiles = swap_chunks([landed[xx * 8 + zz, pair * 2 + low] for low in range(2) for zz in range(8)])
        for high in range(2):
            for frame in range(8):
                now = tiles[high * 8 + frame]
                if frame < 7:
                    later = tiles[high * 8 + frame + 1]
                else:
                    later = pltpu.roll(tiles[high * 8], 4, 0)
                first = high * 64 + frame
                result[block, pl.ds(first, 4, stride=16), :] = (now * (1.0 / (FSUM * 8)))[0:4]
                result[block, pl.ds(first + 8, 4, stride=16), :] = ((now + later) * (1.0 / (FSUM * 16)))[0:4]
        write = pltpu.make_async_copy(result.at[block], out_ref.at[:, pl.ds(block * LANES, LANES)], out_sem.at[block])
        write.start()
        writes.append(write)

    pltpu.make_async_copy(own_ref.at[0:15], own_ref.at[0:15], near_send).wait()
    for flag, index, rows in ((early_self, 0, 8), (late_self, 1, 4)):
        @pl.when(flag)
        def _():
            wait_for(packed, far_send.at[index], 7, rows)

        @pl.when(jnp.logical_not(flag))
        def _():
            wait_for(packed, far_send.at[index], 8, rows)

    for write in writes:
        write.wait()


def search(voltages, feed_slot, tree_shift):
    level = pltpu.VMEM((2, 8, 24, LANES), jnp.float32)
    dma = pltpu.SemaphoreType.DMA
    return pl.pallas_call(
        search_kernel,
        out_shape=jax.ShapeDtypeStruct((8 * BOXES * FRAMES, 512), jnp.float32),
        in_specs=[pl.BlockSpec(memory_space=pltpu.HBM)] * 4,
        out_specs=pl.BlockSpec(memory_space=pl.ANY),
        scratch_shapes=[
            pltpu.SMEM((FEEDS // LANES, LANES), jnp.int32),
            pltpu.VMEM((FEEDS // LANES, LANES), jnp.int32),
            pltpu.SMEM((FEEDS // LANES, LANES), jnp.int32),
            pltpu.SMEM((14,), jnp.int32),
            pltpu.VMEM((2 * SAMPLES, FEEDS), jnp.bfloat16),
            pltpu.VMEM((NS, 2 * NS), jnp.float32),
            pltpu.VMEM((FEEDS * 8, LANES), jnp.float32),
            pltpu.VMEM((FEEDS * 8, LANES), jnp.float32),
            pltpu.VMEM((POL * EW, 2 * NS, SAMPLES), jnp.float32),
            pltpu.VMEM((MEMBERS, 16, LANES), jnp.float32),
            pltpu.VMEM((MEMBERS, 16, LANES), jnp.float32),
            level,
            level,
            level,
            pltpu.VMEM((2, 128, LANES), jnp.float32),
            pltpu.VMEM((8, 4, 8, LANES), jnp.float32),
            pltpu.VMEM((16, 4, 8, LANES), jnp.float32),
            pltpu.VMEM((4, 128, LANES), jnp.float32),
            dma,
            dma,
            dma,
            dma((4,)),
            dma,
            dma,
            dma,
            dma((2,)),
            dma,
            dma,
            dma((4,)),
        ],
        compiler_params=pltpu.CompilerParams(
            collective_id=0, has_side_effects=True, vmem_limit_bytes=60 * 2**20
        ),
        name="search",
    )(
        feed_slot.reshape(FEEDS // LANES, LANES),
        tree_shift,
        voltages.reshape(2 * SAMPLES, FEEDS),
        steer_tables(),
    )


def on_device(voltages, feed_slot, tree_shift):
    result = search(voltages, feed_slot, tree_shift)
    return result.reshape(8, BOXES, FRAMES, 512)


def solution(mesh):
    placed = (P(None, "tm", "beam", None), P(), P())
    return jax.shard_map(
        on_device,
        mesh=mesh,
        in_specs=placed,
        out_specs=P("beam", None, "tm", None),
        check_vma=False,
    )
```

```python
import math

import jax
import jax.numpy as jnp
import ml_dtypes
import numpy as np
from jax import lax
from jax.experimental import pallas as pl
from jax.experimental.pallas import tpu as pltpu
from jax.sharding import PartitionSpec as P

POL = 2
EW = 4
NS = 256
FEEDS = 2048
FSUM = 16
LEVELS = 3
BOXES = 2
FRAMES = 8
CHANS = 64
SAMPLES = FRAMES * CHANS
BANDS = CHANS // FSUM
MEMBERS = 16
SPLIT = 8
LANES = 128
MESH = pl.DeviceIdType.MESH


def steer_table():
    index = np.arange(NS)
    phase = (index[:, None] * index[None, :]) % NS
    angle = phase.astype(np.float32) * np.float32(2.0 * math.pi / NS)
    table = np.concatenate([np.cos(angle)[: NS // 2 + 1], np.sin(angle)[1 : NS // 2]], axis=0)
    return jnp.asarray(table.astype(ml_dtypes.bfloat16).astype(np.float32))


def contract_last(left, right):
    return lax.dot_general(left, right, (((1,), (1,)), ((), ())), preferred_element_type=jnp.float32)


def iota(shape, dim):
    return lax.broadcasted_iota(jnp.int32, shape, dim)


def four_points(re, im):
    even_re, even_im = re[0] + re[2], im[0] + im[2]
    odd_re, odd_im = re[0] - re[2], im[0] - im[2]
    side_re, side_im = re[1] + re[3], im[1] + im[3]
    diff_re, diff_im = re[1] - re[3], im[1] - im[3]
    return [
        (even_re + side_re, even_im + side_im),
        (odd_re + diff_im, odd_im - diff_re),
        (even_re - side_re, even_im - side_im),
        (odd_re - diff_im, odd_im + diff_re),
    ]


def swap_chunks(tiles):
    lane = lax.broadcasted_iota(jnp.int32, (8, LANES), 1)
    tiles = list(tiles)
    for bit in range(4):
        span = 8 << bit
        low_half = (lane // span) % 2 == 0
        for first in range(16):
            if first >> bit & 1:
                continue
            second = first | 1 << bit
            one, two = tiles[first], tiles[second]
            tiles[first] = jnp.where(low_half, one, pltpu.roll(two, span, 1))
            tiles[second] = jnp.where(low_half, pltpu.roll(one, LANES - span, 1), two)
    return tiles


def search_kernel(
    slot_hbm, shift_hbm, volt_hbm, table_hbm, out_ref,
    slot, owner_vmem, owner, shift_ref, volts, table, turned, gridded, north, power, highs, rests,
    own_ref, near, level_0, level_1, level_2, series, packed, landed, result,
    slot_sem, owner_sem, shift_sem, volt_sem, steer_sem,
    near_send, near_recv, far_send, far_recv, self_sem, out_sem,
):
    slot_copy = pltpu.make_async_copy(slot_hbm, slot, slot_sem)
    steer_copy = pltpu.make_async_copy(table_hbm, table, steer_sem)
    shift_copy = pltpu.make_async_copy(shift_hbm, shift_ref, shift_sem)
    volt_copies = [
        pltpu.make_async_copy(
            volt_hbm.at[pl.ds(part * 1024 // SPLIT, 1024 // SPLIT)],
            volts.at[pl.ds(part * 1024 // SPLIT, 1024 // SPLIT)],
            volt_sem.at[part],
        )
        for part in range(SPLIT)
    ]
    for copy in [slot_copy] + volt_copies + [steer_copy, shift_copy]:
        copy.start()

    landed[:, :, 4:8, :] = jnp.zeros((16, 4, 4, LANES), jnp.float32)
    for buffer in (level_0, level_1, level_2):
        buffer[:, :, 16:24, :] = jnp.zeros((2, 8, 8, LANES), jnp.float32)
    place = lax.axis_index("beam")
    half = lax.axis_index("tm")
    core = lax.rem(place, 2)
    site = lax.div(place, 2)
    z = lax.rem(site, 8)
    y = lax.rem(lax.div(site, 8), 4)
    x_high = lax.div(site, 32)
    member = (core * 2 + half) * 4 + y
    selfish = x_high == half

    def of_member(other):
        c, h, at = lax.div(other, 8), lax.rem(lax.div(other, 4), 2), lax.rem(other, 4)
        return (((x_high * 4 + at) * 8 + z) * 2 + c, h)

    def at_site(xx, zz, h):
        return (((xx * 4 + y) * 8 + zz) * 2 + core, h)

    barrier = pltpu.get_barrier_semaphore()

    def greet(step, carry):
        pl.semaphore_signal(
            barrier, inc=1, device_id=of_member(lax.rem(member + step, MEMBERS)), device_id_type=MESH
        )
        return carry

    lax.fori_loop(1, MEMBERS, greet, 0)

    def greet_far(step, carry):
        xx, zz = lax.div(step, 8), lax.rem(z + step, 8)

        @pl.when(jnp.logical_not(jnp.logical_and(jnp.logical_and(xx == x_high, zz == z), selfish)))
        def _():
            pl.semaphore_signal(barrier, inc=1, device_id=at_site(xx, zz, x_high), device_id_type=MESH)

        return carry

    lax.fori_loop(0, 16, greet_far, 0)
    slot_copy.wait()
    places = iota((FEEDS // LANES, LANES), 0) * LANES + iota((FEEDS // LANES, LANES), 1)
    found = [jnp.zeros((FEEDS // LANES, LANES), jnp.int32) for _ in range(4)]
    for feed in range(FEEDS):
        found[feed % 4] = jnp.where(places == slot[feed // LANES, feed % LANES], feed, found[feed % 4])
    owner_vmem[...] = jnp.maximum(jnp.maximum(found[0], found[1]), jnp.maximum(found[2], found[3]))
    owner_copy = pltpu.make_async_copy(owner_vmem, owner, owner_sem)
    owner_copy.start()

    for part in range(4):
        for piece in range(SPLIT // 4):
            volt_copies[part * (SPLIT // 4) + piece].wait()
        for block in range(8):
            flipped = jnp.transpose(volts[pl.ds(part * 256, 256), block * 256 : block * 256 + 256]).astype(jnp.float32)
            for half_rows in range(2):
                turned[pl.ds(block * 2048 + part * 2 + half_rows, 256, stride=8), :] = flipped[
                    :, half_rows * LANES : half_rows * LANES + LANES
                ]

    steer_copy.wait()
    steer = table[...].astype(jnp.bfloat16)
    owner_copy.wait()
    def gather(branch):
        for place in range(NS):
            at = branch * NS + place
            feed = owner[at // LANES, at % LANES]
            gridded[branch][pl.ds(place * 8, 8), :] = turned[pl.ds(feed * 8, 8), :]

    def transform(branch):
        data = [gridded[branch][pl.ds(q, NS, stride=8), :].astype(jnp.bfloat16) for q in range(8)]
        north[branch] = jnp.dot(steer, jnp.concatenate(data, axis=1), preferred_element_type=jnp.float32)

    first_row = iota((16, LANES), 0) == 0

    def energy(pol, strip):
        plus_rows, minus_rows = slice(strip * 16, strip * 16 + 16), slice(128 + strip * 16, 144 + strip * 16)
        for chunk in range(4):
            reals, imags = slice(chunk * LANES, chunk * LANES + LANES), slice(512 + chunk * LANES, 640 + chunk * LANES)
            at = pol * EW
            even = four_points(
                [north[at + e, plus_rows, reals] for e in range(EW)],
                [north[at + e, plus_rows, imags] for e in range(EW)],
            )
            odd = four_points(
                [north[at + e, minus_rows, reals] for e in range(EW)],
                [north[at + e, minus_rows, imags] for e in range(EW)],
            )
            for column in range(EW):
                (even_re, even_im), (odd_re, odd_im) = even[column], odd[column]
                plus_re, plus_im = even_re + odd_im, even_im - odd_re
                minus_re, minus_im = even_re - odd_im, even_im + odd_re
                if strip == 0:
                    plus_re, plus_im = jnp.where(first_row, even_re, plus_re), jnp.where(first_row, even_im, plus_im)
                    minus_re, minus_im = jnp.where(first_row, odd_re, minus_re), jnp.where(first_row, odd_im, minus_im)
                plus = plus_re * plus_re + plus_im * plus_im
                minus = minus_re * minus_re + minus_im * minus_im
                for first, part in ((strip * 32, plus), (strip * 32 + 16, minus)):
                    rows = slice(first, first + 16)
                    if pol == 0:
                        power[column, rows, reals] = part
                    else:
                        part = part + power[column, rows, reals]
                        high = part.astype(jnp.bfloat16)
                        highs[column, rows, reals] = high
                        rests[column, rows, reals] = (part - high.astype(jnp.float32)).astype(jnp.bfloat16)

    gather(0)
    for branch in range(POL * EW):
        if branch + 1 < POL * EW:
            gather(branch + 1)
        transform(branch)
        if branch >= EW:
            energy(0, 2 * (branch - EW))
            energy(0, 2 * (branch - EW) + 1)

    for strip in range(8):
        energy(1, strip)
    sample, place = iota((SAMPLES, LANES), 0), iota((SAMPLES, LANES), 1)
    chosen = (sample // CHANS == place % FRAMES) & (sample % CHANS // FSUM == place // FRAMES % BANDS)
    sums = jnp.zeros((NS, LANES), jnp.float32)
    for column in range(EW):
        own = chosen & (place // (BANDS * FRAMES) == column)
        adder = jnp.where(own, 0.5 / FEEDS, 0.0).astype(jnp.bfloat16)
        sums = sums + jnp.dot(highs[column], adder, preferred_element_type=jnp.float32)
        sums = sums + jnp.dot(rests[column], adder, preferred_element_type=jnp.float32)
    lane, source = iota((NS, NS), 1), iota((NS, NS), 0)
    output = lane // 8 % 16 * 16 + lane // 128 * 8 + lane % 8
    folded = jnp.where(output < 128, output, (256 - output) % 128)
    home = folded // 16 * 32 + folded % 16 + jnp.where(output < 128, 0, 16)
    order = jnp.where(source == home, 1.0, 0.0).astype(jnp.bfloat16)
    low_lanes = iota((16, LANES), 1) < LANES // 2
    binned = jnp.transpose(sums)
    high = binned.astype(jnp.bfloat16)
    rest = (binned - high.astype(jnp.float32)).astype(jnp.bfloat16)
    binned = jnp.dot(high, order, preferred_element_type=jnp.float32) + jnp.dot(
        rest, order, preferred_element_type=jnp.float32
    )
    for column in range(EW):
        for c in range(2):
            lanes = slice(c * LANES, c * LANES + LANES)
            one, two = binned[column * 32 : column * 32 + 16, lanes], binned[column * 32 + 16 : column * 32 + 32, lanes]
            target = (c * 2 + column // 2) * 4 + column % 2 * 2
            own_ref[target] = jnp.where(low_lanes, one, pltpu.roll(two, LANES // 2, 1))
            own_ref[target + 1] = jnp.where(low_lanes, pltpu.roll(one, LANES // 2, 1), two)

    pl.semaphore_wait(barrier, jnp.where(selfish, MEMBERS + 14, MEMBERS + 15))

    def near_copy(other):
        return pltpu.make_async_remote_copy(
            src_ref=own_ref.at[other],
            dst_ref=near.at[member],
            send_sem=near_send,
            recv_sem=near_recv,
            device_id=of_member(other),
            device_id_type=MESH,
        )

    def send_near(step, carry):
        near_copy(lax.rem(member + step, MEMBERS)).start()
        return carry

    lax.fori_loop(1, MEMBERS, send_near, 0)
    mine = pltpu.make_async_copy(own_ref.at[member], near.at[member], self_sem)
    mine.start()
    mine.wait()
    pltpu.make_async_copy(near.at[0:15], near.at[0:15], near_recv).wait()

    shift_copy.wait()
    low_frames = iota((FRAMES, LANES), 1) < LANES // 2
    for c in range(2):
        for h in range(2):
            for pair in range(2):
                first = (c * 2 + h) * 4 + pair * 2
                for low in range(2):
                    one, two = near[first, low * 8 : low * 8 + 8, :], near[first + 1, low * 8 : low * 8 + 8, :]
                    frames = slice(h * 8, h * 8 + 8)
                    level_0[pair, c * 4 + low, frames, :] = jnp.where(low_frames, one, pltpu.roll(two, LANES // 2, 1))
                    level_0[pair, c * 4 + 2 + low, frames, :] = jnp.where(
                        low_frames, pltpu.roll(one, LANES // 2, 1), two
                    )

    buffers = (level_0, level_1, level_2)
    for level in range(LEVELS):
        span = 2**level
        current = buffers[level]
        for band in range(8):
            base, k = band - band % (2 * span), band % (2 * span)
            lower = base + k // 2
            lag = shift_ref[2 * span - 2 + k]
            for pair in range(2):
                total = current[pair, lower, 0:16, :] + current[pair, lower + span, pl.ds(lag, 16), :]
                if level < LEVELS - 1:
                    buffers[level + 1][pair, band, 0:16, :] = total
                else:
                    series[pair, pl.ds(band, 16, stride=8), :] = total
    keep = (iota((8, LANES), 1) < LANES // 2) == (iota((8, LANES), 0) < 4)
    for pair in range(2):
        flipped = jnp.transpose(series[pair])
        for low in range(2):
            for target in range(8):
                first = low * 64 + target * 8
                tile = flipped[first : first + 8]
                crossed = pltpu.roll(pltpu.roll(tile, 4, 0), LANES // 2, 1)
                packed[target, pair * 2 + low] = jnp.where(keep, tile, crossed)

    slot = x_high * 8 + z

    def to_early(target):
        return pltpu.make_async_remote_copy(
            src_ref=packed.at[target],
            dst_ref=landed.at[slot],
            send_sem=far_send.at[0],
            recv_sem=far_recv,
            device_id=at_site(half, target, 0),
            device_id_type=MESH,
        )

    def to_late(target):
        return pltpu.make_async_remote_copy(
            src_ref=packed.at[target, :, 4:8],
            dst_ref=landed.at[slot, :, 0:4],
            send_sem=far_send.at[1],
            recv_sem=far_recv,
            device_id=at_site(half, target, 1),
            device_id_type=MESH,
        )

    early_self = jnp.logical_and(selfish, half == 0)
    late_self = jnp.logical_and(selfish, half == 1)

    def send(step, carry):
        target = lax.rem(z + step, 8)

        @pl.when(jnp.logical_not(jnp.logical_and(target == z, early_self)))
        def _():
            to_early(target).start()

        @pl.when(jnp.logical_not(jnp.logical_and(target == z, late_self)))
        def _():
            to_late(target).start()

        return carry

    lax.fori_loop(0, 8, send, 0)

    @pl.when(early_self)
    def _():
        copy = pltpu.make_async_copy(packed.at[z], landed.at[slot], self_sem)
        copy.start()
        copy.wait()

    @pl.when(late_self)
    def _():
        copy = pltpu.make_async_copy(packed.at[z, :, 4:8], landed.at[slot, :, 0:4], self_sem)
        copy.start()
        copy.wait()

    def wait_for(buffer, sem, count, rows):
        part = buffer.at[0:count, :, 0:rows]
        pltpu.make_async_copy(part, part, sem).wait()

    for h, rows in ((0, 8), (1, 4)):
        @pl.when(jnp.logical_and(half == h, selfish))
        def _():
            wait_for(landed, far_recv, 15, rows)

        @pl.when(jnp.logical_and(half == h, jnp.logical_not(selfish)))
        def _():
            wait_for(landed, far_recv, 16, rows)

    writes = []
    for block in range(4):
        xx, pair = block // 2, block % 2
        tiles = swap_chunks([landed[xx * 8 + zz, pair * 2 + low] for low in range(2) for zz in range(8)])
        for high in range(2):
            for frame in range(8):
                now = tiles[high * 8 + frame]
                if frame < 7:
                    later = tiles[high * 8 + frame + 1]
                else:
                    later = pltpu.roll(tiles[high * 8], 4, 0)
                first = high * 64 + frame
                result[block, pl.ds(first, 4, stride=16), :] = (now * (1.0 / (FSUM * 8)))[0:4]
                result[block, pl.ds(first + 8, 4, stride=16), :] = ((now + later) * (1.0 / (FSUM * 16)))[0:4]
        write = pltpu.make_async_copy(result.at[block], out_ref.at[:, pl.ds(block * LANES, LANES)], out_sem.at[block])
        write.start()
        writes.append(write)

    pltpu.make_async_copy(own_ref.at[0:15], own_ref.at[0:15], near_send).wait()
    for flag, index, rows in ((early_self, 0, 8), (late_self, 1, 4)):
        @pl.when(flag)
        def _():
            wait_for(packed, far_send.at[index], 7, rows)

        @pl.when(jnp.logical_not(flag))
        def _():
            wait_for(packed, far_send.at[index], 8, rows)

    for write in writes:
        write.wait()


def search(voltages, feed_slot, tree_shift):
    level = pltpu.VMEM((2, 8, 24, LANES), jnp.float32)
    dma = pltpu.SemaphoreType.DMA
    return pl.pallas_call(
        search_kernel,
        out_shape=jax.ShapeDtypeStruct((8 * BOXES * FRAMES, 512), jnp.float32),
        in_specs=[pl.BlockSpec(memory_space=pltpu.HBM)] * 4,
        out_specs=pl.BlockSpec(memory_space=pl.ANY),
        scratch_shapes=[
            pltpu.SMEM((FEEDS // LANES, LANES), jnp.int32),
            pltpu.VMEM((FEEDS // LANES, LANES), jnp.int32),
            pltpu.SMEM((FEEDS // LANES, LANES), jnp.int32),
            pltpu.SMEM((14,), jnp.int32),
            pltpu.VMEM((2 * SAMPLES, FEEDS), jnp.bfloat16),
            pltpu.VMEM((NS, NS), jnp.float32),
            pltpu.VMEM((FEEDS * 8, LANES), jnp.float32),
            [pltpu.VMEM((NS * 8, LANES), jnp.float32)] * (POL * EW),
            pltpu.VMEM((POL * EW, NS, 2 * SAMPLES), jnp.float32),
            pltpu.VMEM((EW, NS, SAMPLES), jnp.float32),
            pltpu.VMEM((EW, NS, SAMPLES), jnp.bfloat16),
            pltpu.VMEM((EW, NS, SAMPLES), jnp.bfloat16),
            pltpu.VMEM((MEMBERS, 16, LANES), jnp.float32),
            pltpu.VMEM((MEMBERS, 16, LANES), jnp.float32),
            level,
            level,
            level,
            pltpu.VMEM((2, 128, LANES), jnp.float32),
            pltpu.VMEM((8, 4, 8, LANES), jnp.float32),
            pltpu.VMEM((16, 4, 8, LANES), jnp.float32),
            pltpu.VMEM((4, 128, LANES), jnp.float32),
            dma,
            dma,
            dma,
            dma((SPLIT,)),
            dma,
            dma,
            dma,
            dma((2,)),
            dma,
            dma,
            dma((4,)),
        ],
        compiler_params=pltpu.CompilerParams(
            collective_id=0, has_side_effects=True, vmem_limit_bytes=60 * 2**20
        ),
        name="search",
    )(
        feed_slot.reshape(FEEDS // LANES, LANES),
        tree_shift,
        voltages.reshape(2 * SAMPLES, FEEDS),
        steer_table(),
    )


def on_device(voltages, feed_slot, tree_shift):
    result = search(voltages, feed_slot, tree_shift)
    return result.reshape(8, BOXES, FRAMES, 512)


def solution(mesh):
    placed = (P(None, "tm", "beam", None), P(), P())
    return jax.shard_map(
        on_device,
        mesh=mesh,
        in_specs=placed,
        out_specs=P("beam", None, "tm", None),
        check_vma=False,
    )
```

```python
import itertools
import math

import jax
import jax.numpy as jnp
import ml_dtypes
import numpy as np
from jax import lax
from jax.experimental import pallas as pl
from jax.experimental.pallas import tpu as pltpu
from jax.sharding import PartitionSpec as P

POL = 2
EW = 4
NS = 256
FEEDS = 2048
FSUM = 16
LEVELS = 3
BOXES = 2
FRAMES = 8
CHANS = 64
SAMPLES = FRAMES * CHANS
BANDS = CHANS // FSUM
MEMBERS = 16
SPLIT = 8
LANES = 128
MESH = pl.DeviceIdType.MESH


def steer_table():
    index = np.arange(NS)
    phase = (index[:, None] * index[None, :]) % NS
    angle = phase.astype(np.float32) * np.float32(2.0 * math.pi / NS)
    table = np.concatenate([np.cos(angle)[: NS // 2 + 1], np.sin(angle)[1 : NS // 2]], axis=0)
    return jnp.asarray(table.astype(ml_dtypes.bfloat16).astype(np.float32))


def contract_last(left, right):
    return lax.dot_general(left, right, (((1,), (1,)), ((), ())), preferred_element_type=jnp.float32)


def iota(shape, dim):
    return lax.broadcasted_iota(jnp.int32, shape, dim)


def four_points(re, im):
    even_re, even_im = re[0] + re[2], im[0] + im[2]
    odd_re, odd_im = re[0] - re[2], im[0] - im[2]
    side_re, side_im = re[1] + re[3], im[1] + im[3]
    diff_re, diff_im = re[1] - re[3], im[1] - im[3]
    return [
        (even_re + side_re, even_im + side_im),
        (odd_re + diff_im, odd_im - diff_re),
        (even_re - side_re, even_im - side_im),
        (odd_re - diff_im, odd_im + diff_re),
    ]


def swap_chunks(tiles):
    lane = lax.broadcasted_iota(jnp.int32, (8, LANES), 1)
    tiles = list(tiles)
    for bit in range(4):
        span = 8 << bit
        low_half = (lane // span) % 2 == 0
        for first in range(16):
            if first >> bit & 1:
                continue
            second = first | 1 << bit
            one, two = tiles[first], tiles[second]
            tiles[first] = jnp.where(low_half, one, pltpu.roll(two, span, 1))
            tiles[second] = jnp.where(low_half, pltpu.roll(one, LANES - span, 1), two)
    return tiles


def search_kernel(
    slot_hbm, shift_hbm, volt_hbm, table_hbm, landed,
    slot, owner_vmem, owner, shift_ref, volts, table, turned, gridded, north, power, highs, rests,
    own_ref, near, level_0, level_1, level_2, series, early, late,
    slot_sem, owner_sem, shift_sem, volt_sem, steer_sem,
    near_send, near_recv, far_send, far_recv, self_sem,
):
    slot_copy = pltpu.make_async_copy(slot_hbm, slot, slot_sem)
    steer_copy = pltpu.make_async_copy(table_hbm, table, steer_sem)
    shift_copy = pltpu.make_async_copy(shift_hbm, shift_ref, shift_sem)
    volt_copies = [
        pltpu.make_async_copy(
            volt_hbm.at[pl.ds(part * 1024 // SPLIT, 1024 // SPLIT)],
            volts.at[pl.ds(part * 1024 // SPLIT, 1024 // SPLIT)],
            volt_sem.at[part],
        )
        for part in range(SPLIT)
    ]
    for copy in [slot_copy] + volt_copies + [steer_copy, shift_copy]:
        copy.start()

    for buffer in (level_0, level_1, level_2):
        buffer[:, :, 16:24, :] = jnp.zeros((2, 8, 8, LANES), jnp.float32)
    place = lax.axis_index("beam")
    half = lax.axis_index("tm")
    core = lax.rem(place, 2)
    site = lax.div(place, 2)
    z = lax.rem(site, 8)
    y = lax.rem(lax.div(site, 8), 4)
    x_high = lax.div(site, 32)
    member = (core * 2 + half) * 4 + y
    selfish = x_high == half

    def of_member(other):
        c, h, at = lax.div(other, 8), lax.rem(lax.div(other, 4), 2), lax.rem(other, 4)
        return (((x_high * 4 + at) * 8 + z) * 2 + c, h)

    def at_site(xx, zz, h):
        return (((xx * 4 + y) * 8 + zz) * 2 + core, h)

    barrier = pltpu.get_barrier_semaphore()

    def greet(step, carry):
        pl.semaphore_signal(
            barrier, inc=1, device_id=of_member(lax.rem(member + step, MEMBERS)), device_id_type=MESH
        )
        return carry

    lax.fori_loop(1, MEMBERS, greet, 0)

    def greet_far(step, carry):
        xx, zz = lax.div(step, 8), lax.rem(z + step, 8)

        @pl.when(jnp.logical_not(jnp.logical_and(jnp.logical_and(xx == x_high, zz == z), selfish)))
        def _():
            pl.semaphore_signal(barrier, inc=1, device_id=at_site(xx, zz, x_high), device_id_type=MESH)

        return carry

    lax.fori_loop(0, 16, greet_far, 0)
    slot_copy.wait()
    places = iota((FEEDS // LANES, LANES), 0) * LANES + iota((FEEDS // LANES, LANES), 1)
    found = [jnp.zeros((FEEDS // LANES, LANES), jnp.int32) for _ in range(4)]
    for feed in range(FEEDS):
        found[feed % 4] = jnp.where(places == slot[feed // LANES, feed % LANES], feed, found[feed % 4])
    owner_vmem[...] = jnp.maximum(jnp.maximum(found[0], found[1]), jnp.maximum(found[2], found[3]))
    owner_copy = pltpu.make_async_copy(owner_vmem, owner, owner_sem)
    owner_copy.start()

    for part in range(4):
        for piece in range(SPLIT // 4):
            volt_copies[part * (SPLIT // 4) + piece].wait()
        for block in range(8):
            flipped = jnp.transpose(volts[pl.ds(part * 256, 256), block * 256 : block * 256 + 256]).astype(jnp.float32)
            for half_rows in range(2):
                turned[pl.ds(block * 2048 + part * 2 + half_rows, 256, stride=8), :] = flipped[
                    :, half_rows * LANES : half_rows * LANES + LANES
                ]

    steer_copy.wait()
    steer = table[...].astype(jnp.bfloat16)
    owner_copy.wait()
    def gather(branch):
        for place in range(NS):
            at = branch * NS + place
            feed = owner[at // LANES, at % LANES]
            gridded[branch][pl.ds(place * 8, 8), :] = turned[pl.ds(feed * 8, 8), :]

    def transform(branch):
        data = [gridded[branch][pl.ds(q, NS, stride=8), :].astype(jnp.bfloat16) for q in range(8)]
        north[branch] = jnp.dot(steer, jnp.concatenate(data, axis=1), preferred_element_type=jnp.float32)

    first_row = iota((16, LANES), 0) == 0

    def energy(pol, strip):
        plus_rows, minus_rows = slice(strip * 16, strip * 16 + 16), slice(128 + strip * 16, 144 + strip * 16)
        for chunk in range(4):
            reals, imags = slice(chunk * LANES, chunk * LANES + LANES), slice(512 + chunk * LANES, 640 + chunk * LANES)
            at = pol * EW
            even = four_points(
                [north[at + e, plus_rows, reals] for e in range(EW)],
                [north[at + e, plus_rows, imags] for e in range(EW)],
            )
            odd = four_points(
                [north[at + e, minus_rows, reals] for e in range(EW)],
                [north[at + e, minus_rows, imags] for e in range(EW)],
            )
            for column in range(EW):
                (even_re, even_im), (odd_re, odd_im) = even[column], odd[column]
                plus_re, plus_im = even_re + odd_im, even_im - odd_re
                minus_re, minus_im = even_re - odd_im, even_im + odd_re
                if strip == 0:
                    plus_re, plus_im = jnp.where(first_row, even_re, plus_re), jnp.where(first_row, even_im, plus_im)
                    minus_re, minus_im = jnp.where(first_row, odd_re, minus_re), jnp.where(first_row, odd_im, minus_im)
                plus = plus_re * plus_re + plus_im * plus_im
                minus = minus_re * minus_re + minus_im * minus_im
                for first, part in ((strip * 32, plus), (strip * 32 + 16, minus)):
                    rows = slice(first, first + 16)
                    if pol == 0:
                        power[column, rows, reals] = part
                    else:
                        part = part + power[column, rows, reals]
                        high = part.astype(jnp.bfloat16)
                        highs[column, rows, reals] = high
                        rests[column, rows, reals] = (part - high.astype(jnp.float32)).astype(jnp.bfloat16)

    gather(0)
    for branch in range(POL * EW):
        if branch + 1 < POL * EW:
            gather(branch + 1)
        transform(branch)
        if branch >= EW:
            energy(0, 2 * (branch - EW))
            energy(0, 2 * (branch - EW) + 1)

    for strip in range(8):
        energy(1, strip)
    sample, place = iota((SAMPLES, LANES), 0), iota((SAMPLES, LANES), 1)
    chosen = (sample // CHANS == place % FRAMES) & (sample % CHANS // FSUM == place // FRAMES % BANDS)
    sums = jnp.zeros((NS, LANES), jnp.float32)
    for column in range(EW):
        own = chosen & (place // (BANDS * FRAMES) == column)
        adder = jnp.where(own, 0.5 / FEEDS, 0.0).astype(jnp.bfloat16)
        sums = sums + jnp.dot(highs[column], adder, preferred_element_type=jnp.float32)
        sums = sums + jnp.dot(rests[column], adder, preferred_element_type=jnp.float32)
    lane, source = iota((NS, NS), 1), iota((NS, NS), 0)
    output = lane // 8 % 16 * 16 + lane // 128 * 8 + lane % 8
    folded = jnp.where(output < 128, output, (256 - output) % 128)
    home = folded // 16 * 32 + folded % 16 + jnp.where(output < 128, 0, 16)
    order = jnp.where(source == home, 1.0, 0.0).astype(jnp.bfloat16)
    low_lanes = iota((16, LANES), 1) < LANES // 2
    binned = jnp.transpose(sums)
    high = binned.astype(jnp.bfloat16)
    rest = (binned - high.astype(jnp.float32)).astype(jnp.bfloat16)
    binned = jnp.dot(high, order, preferred_element_type=jnp.float32) + jnp.dot(
        rest, order, preferred_element_type=jnp.float32
    )
    for column in range(EW):
        for c in range(2):
            lanes = slice(c * LANES, c * LANES + LANES)
            one, two = binned[column * 32 : column * 32 + 16, lanes], binned[column * 32 + 16 : column * 32 + 32, lanes]
            target = (c * 2 + column // 2) * 4 + column % 2 * 2
            own_ref[target] = jnp.where(low_lanes, one, pltpu.roll(two, LANES // 2, 1))
            own_ref[target + 1] = jnp.where(low_lanes, pltpu.roll(one, LANES // 2, 1), two)

    pl.semaphore_wait(barrier, jnp.where(selfish, MEMBERS + 14, MEMBERS + 15))

    def near_copy(other):
        return pltpu.make_async_remote_copy(
            src_ref=own_ref.at[other],
            dst_ref=near.at[member],
            send_sem=near_send,
            recv_sem=near_recv,
            device_id=of_member(other),
            device_id_type=MESH,
        )

    for dy, dx, dc in itertools.product((2, 1, 3, 0), (1, 0), (1, 0)):
        if dy + dx + dc > 0:
            near_copy((lax.rem(core + dc, 2) * 2 + lax.rem(half + dx, 2)) * 4 + lax.rem(y + dy, 4)).start()
    mine = pltpu.make_async_copy(own_ref.at[member], near.at[member], self_sem)
    mine.start()
    mine.wait()
    pltpu.make_async_copy(near.at[0:15], near.at[0:15], near_recv).wait()

    shift_copy.wait()
    low_frames = iota((FRAMES, LANES), 1) < LANES // 2
    for c in range(2):
        for h in range(2):
            for pair in range(2):
                first = (c * 2 + h) * 4 + pair * 2
                for low in range(2):
                    one, two = near[first, low * 8 : low * 8 + 8, :], near[first + 1, low * 8 : low * 8 + 8, :]
                    frames = slice(h * 8, h * 8 + 8)
                    level_0[pair, c * 4 + low, frames, :] = jnp.where(low_frames, one, pltpu.roll(two, LANES // 2, 1))
                    level_0[pair, c * 4 + 2 + low, frames, :] = jnp.where(
                        low_frames, pltpu.roll(one, LANES // 2, 1), two
                    )

    buffers = (level_0, level_1, level_2)
    for level in range(LEVELS):
        span = 2**level
        current = buffers[level]
        for band in range(8):
            base, k = band - band % (2 * span), band % (2 * span)
            lower = base + k // 2
            lag = shift_ref[2 * span - 2 + k]
            for pair in range(2):
                total = current[pair, lower, 0:16, :] + current[pair, lower + span, pl.ds(lag, 16), :]
                if level < LEVELS - 1:
                    buffers[level + 1][pair, band, 0:16, :] = total
                else:
                    series[pair, pl.ds(band, 16, stride=8), :] = total
    low_half = iota((8, LANES), 1) < LANES // 2
    low_rows = iota((8, LANES), 0) < 4
    chunk = iota((8, LANES), 1) // 8
    ninth = [jnp.zeros((8, LANES), jnp.float32) for _ in range(8)]
    for pair in range(2):
        flipped = jnp.transpose(series[pair])
        for target in range(8):
            for low in range(2):
                tile = flipped[low * 64 + target * 8 : low * 64 + target * 8 + 8]
                at = pair * 2 + low
                crossed = pltpu.roll(pltpu.roll(tile, 4, 0), LANES // 2, 1)
                both = jnp.where(low_half == low_rows, tile, crossed)
                early[target, at * 4 : at * 4 + 4, :] = both[0:4]
                late[target, at * 4 : at * 4 + 4, :] = both[4:8]
                ninth[target] = jnp.where(chunk == at, pltpu.roll(tile, LANES // 2 + at * 8, 1), ninth[target])
    for target in range(8):
        early[target, 16:24, :] = ninth[target]

    source = x_high * 8 + z

    def to_early(target):
        return pltpu.make_async_remote_copy(
            src_ref=early.at[target],
            dst_ref=landed.at[source],
            send_sem=far_send.at[0],
            recv_sem=far_recv,
            device_id=at_site(half, target, 0),
            device_id_type=MESH,
        )

    def to_late(target):
        return pltpu.make_async_remote_copy(
            src_ref=late.at[target],
            dst_ref=landed.at[source, 0:16],
            send_sem=far_send.at[1],
            recv_sem=far_recv,
            device_id=at_site(half, target, 1),
            device_id_type=MESH,
        )

    early_self = jnp.logical_and(selfish, half == 0)
    late_self = jnp.logical_and(selfish, half == 1)
    for dz in (4, 3, 5, 2, 6, 1, 7):
        to_early(lax.rem(z + dz, 8)).start()
        to_late(lax.rem(z + dz, 8)).start()

    @pl.when(jnp.logical_not(early_self))
    def _():
        to_early(z).start()

    @pl.when(jnp.logical_not(late_self))
    def _():
        to_late(z).start()

    @pl.when(early_self)
    def _():
        copy = pltpu.make_async_copy(early.at[z], landed.at[source], self_sem)
        copy.start()
        copy.wait()

    @pl.when(late_self)
    def _():
        copy = pltpu.make_async_copy(late.at[z], landed.at[source, 0:16], self_sem)
        copy.start()
        copy.wait()

    def wait_for(part, sem):
        pltpu.make_async_copy(part, part, sem).wait()

    for h, rows in ((0, 24), (1, 16)):
        @pl.when(jnp.logical_and(half == h, selfish))
        def _():
            wait_for(landed.at[0:15, 0:rows], far_recv)

        @pl.when(jnp.logical_and(half == h, jnp.logical_not(selfish)))
        def _():
            wait_for(landed.at[:, 0:rows], far_recv)

    wait_for(own_ref.at[0:15], near_send)
    for flag, index, buffer in ((early_self, 0, early), (late_self, 1, late)):
        @pl.when(flag)
        def _():
            wait_for(buffer.at[0:7], far_send.at[index])

        @pl.when(jnp.logical_not(flag))
        def _():
            wait_for(buffer, far_send.at[index])


def finish_kernel(landed_hbm, out_ref, landed, result, in_sem, out_sem):
    reads = [
        pltpu.make_async_copy(landed_hbm.at[xx * 8 : xx * 8 + 8], landed.at[xx * 8 : xx * 8 + 8], in_sem.at[xx])
        for xx in range(2)
    ]
    for copy in reads:
        copy.start()
    chunk = iota((8, LANES), 1) // 8
    has_ninth = jnp.broadcast_to(lax.axis_index("tm"), (8, LANES)) == 0
    writes = []
    for xx in range(2):
        reads[xx].wait()
        for pair in range(2):
            block = xx * 2 + pair
            tiles = []
            ninth = jnp.zeros((8, LANES), jnp.float32)
            for low in range(2):
                at = pair * 2 + low
                for zz in range(8):
                    tiles.append(landed[xx * 8 + zz, at * 4 : at * 4 + 8, :])
                    to = low * 8 + zz
                    ninth = jnp.where(
                        chunk == to, pltpu.roll(landed[xx * 8 + zz, 16:24, :], (to - at) * 8 % LANES, 1), ninth
                    )
            ninth = jnp.where(has_ninth, ninth, 0.0)
            tiles = swap_chunks(tiles)
            for high in range(2):
                for frame in range(8):
                    now = tiles[high * 8 + frame][0:4]
                    if frame < 7:
                        later = tiles[high * 8 + frame + 1][0:4]
                    else:
                        later = ninth[high * 4 : high * 4 + 4]
                    first = high * 64 + frame
                    result[block, pl.ds(first, 4, stride=16), :] = now * (1.0 / (FSUM * 8))
                    result[block, pl.ds(first + 8, 4, stride=16), :] = (now + later) * (1.0 / (FSUM * 16))
            write = pltpu.make_async_copy(
                result.at[block], out_ref.at[:, pl.ds(block * LANES, LANES)], out_sem.at[block]
            )
            write.start()
            writes.append(write)
    for write in writes:
        write.wait()


def finish(landed):
    return pl.pallas_call(
        finish_kernel,
        out_shape=jax.ShapeDtypeStruct((8 * BOXES * FRAMES, 512), jnp.float32),
        in_specs=[pl.BlockSpec(memory_space=pltpu.HBM)],
        out_specs=pl.BlockSpec(memory_space=pltpu.HBM),
        scratch_shapes=[
            pltpu.VMEM((16, 24, LANES), jnp.float32),
            pltpu.VMEM((4, 128, LANES), jnp.float32),
            pltpu.SemaphoreType.DMA((2,)),
            pltpu.SemaphoreType.DMA((4,)),
        ],
        compiler_params=pltpu.CompilerParams(vmem_limit_bytes=60 * 2**20),
        name="finish",
    )(landed)


def search(voltages, feed_slot, tree_shift):
    level = pltpu.VMEM((2, 8, 24, LANES), jnp.float32)
    dma = pltpu.SemaphoreType.DMA
    return pl.pallas_call(
        search_kernel,
        out_shape=jax.ShapeDtypeStruct((16, 24, LANES), jnp.float32),
        in_specs=[pl.BlockSpec(memory_space=pltpu.HBM)] * 4,
        out_specs=pl.BlockSpec(memory_space=pltpu.HBM),
        scratch_shapes=[
            pltpu.SMEM((FEEDS // LANES, LANES), jnp.int32),
            pltpu.VMEM((FEEDS // LANES, LANES), jnp.int32),
            pltpu.SMEM((FEEDS // LANES, LANES), jnp.int32),
            pltpu.SMEM((14,), jnp.int32),
            pltpu.VMEM((2 * SAMPLES, FEEDS), jnp.bfloat16),
            pltpu.VMEM((NS, NS), jnp.float32),
            pltpu.VMEM((FEEDS * 8, LANES), jnp.float32),
            [pltpu.VMEM((NS * 8, LANES), jnp.float32)] * (POL * EW),
            pltpu.VMEM((POL * EW, NS, 2 * SAMPLES), jnp.float32),
            pltpu.VMEM((EW, NS, SAMPLES), jnp.float32),
            pltpu.VMEM((EW, NS, SAMPLES), jnp.bfloat16),
            pltpu.VMEM((EW, NS, SAMPLES), jnp.bfloat16),
            pltpu.VMEM((MEMBERS, 16, LANES), jnp.float32),
            pltpu.VMEM((MEMBERS, 16, LANES), jnp.float32),
            level,
            level,
            level,
            pltpu.VMEM((2, 128, LANES), jnp.float32),
            pltpu.VMEM((8, 24, LANES), jnp.float32),
            pltpu.VMEM((8, 16, LANES), jnp.float32),
            dma,
            dma,
            dma,
            dma((SPLIT,)),
            dma,
            dma,
            dma,
            dma((2,)),
            dma,
            dma,
        ],
        compiler_params=pltpu.CompilerParams(
            collective_id=0, has_side_effects=True, vmem_limit_bytes=60 * 2**20
        ),
        name="search",
    )(
        feed_slot.reshape(FEEDS // LANES, LANES),
        tree_shift,
        voltages.reshape(2 * SAMPLES, FEEDS),
        steer_table(),
    )


def on_device(voltages, feed_slot, tree_shift):
    result = finish(search(voltages, feed_slot, tree_shift))
    return result.reshape(8, BOXES, FRAMES, 512)


def solution(mesh):
    placed = (P(None, "tm", "beam", None), P(), P())
    return jax.shard_map(
        on_device,
        mesh=mesh,
        in_specs=placed,
        out_specs=P("beam", None, "tm", None),
        check_vma=False,
    )
```

```python
import itertools
import math

import jax
import jax.numpy as jnp
import ml_dtypes
import numpy as np
from jax import lax
from jax.experimental import pallas as pl
from jax.experimental.pallas import tpu as pltpu
from jax.sharding import PartitionSpec as P

POL = 2
EW = 4
NS = 256
FEEDS = 2048
FSUM = 16
LEVELS = 3
BOXES = 2
FRAMES = 8
CHANS = 64
SAMPLES = FRAMES * CHANS
BANDS = CHANS // FSUM
MEMBERS = 16
SPLIT = 8
LANES = 128
MESH = pl.DeviceIdType.MESH


def steer_table():
    index = np.arange(NS)
    phase = (index[:, None] * index[None, :]) % NS
    angle = phase.astype(np.float32) * np.float32(2.0 * math.pi / NS)
    table = np.concatenate([np.cos(angle)[: NS // 2 + 1], np.sin(angle)[1 : NS // 2]], axis=0)
    return jnp.asarray(table.astype(ml_dtypes.bfloat16).astype(np.float32))


def contract_last(left, right):
    return lax.dot_general(left, right, (((1,), (1,)), ((), ())), preferred_element_type=jnp.float32)


def iota(shape, dim):
    return lax.broadcasted_iota(jnp.int32, shape, dim)


def four_points(re, im):
    even_re, even_im = re[0] + re[2], im[0] + im[2]
    odd_re, odd_im = re[0] - re[2], im[0] - im[2]
    side_re, side_im = re[1] + re[3], im[1] + im[3]
    diff_re, diff_im = re[1] - re[3], im[1] - im[3]
    return [
        (even_re + side_re, even_im + side_im),
        (odd_re + diff_im, odd_im - diff_re),
        (even_re - side_re, even_im - side_im),
        (odd_re - diff_im, odd_im + diff_re),
    ]


def swap_chunks(tiles):
    lane = lax.broadcasted_iota(jnp.int32, (8, LANES), 1)
    tiles = list(tiles)
    for bit in range(4):
        span = 8 << bit
        low_half = (lane // span) % 2 == 0
        for first in range(16):
            if first >> bit & 1:
                continue
            second = first | 1 << bit
            one, two = tiles[first], tiles[second]
            tiles[first] = jnp.where(low_half, one, pltpu.roll(two, span, 1))
            tiles[second] = jnp.where(low_half, pltpu.roll(one, LANES - span, 1), two)
    return tiles


def search_kernel(
    slot_hbm, shift_hbm, volt_hbm, table_hbm, landed,
    slot, owner_vmem, owner, shift_ref, volts, table, turned, gridded, north, power, highs, rests,
    own_ref, near, level_0, level_1, level_2, series, early, late,
    slot_sem, owner_sem, shift_sem, volt_sem, steer_sem,
    near_send, near_recv, far_send, far_recv, self_sem,
):
    slot_copy = pltpu.make_async_copy(slot_hbm, slot, slot_sem)
    steer_copy = pltpu.make_async_copy(table_hbm, table, steer_sem)
    shift_copy = pltpu.make_async_copy(shift_hbm, shift_ref, shift_sem)
    volt_copies = [
        pltpu.make_async_copy(
            volt_hbm.at[pl.ds(part * 1024 // SPLIT, 1024 // SPLIT)],
            volts.at[pl.ds(part * 1024 // SPLIT, 1024 // SPLIT)],
            volt_sem.at[part],
        )
        for part in range(SPLIT)
    ]
    for copy in [slot_copy] + volt_copies + [steer_copy, shift_copy]:
        copy.start()

    for buffer in (level_0, level_1, level_2):
        buffer[:, :, 16:24, :] = jnp.zeros((2, 8, 8, LANES), jnp.float32)
    place = lax.axis_index("beam")
    half = lax.axis_index("tm")
    core = lax.rem(place, 2)
    site = lax.div(place, 2)
    z = lax.rem(site, 8)
    y = lax.rem(lax.div(site, 8), 4)
    x_high = lax.div(site, 32)
    member = (core * 2 + half) * 4 + y
    selfish = x_high == half

    def of_member(other):
        c, h, at = lax.div(other, 8), lax.rem(lax.div(other, 4), 2), lax.rem(other, 4)
        return (((x_high * 4 + at) * 8 + z) * 2 + c, h)

    def at_site(xx, zz, h):
        return (((xx * 4 + y) * 8 + zz) * 2 + core, h)

    barrier = pltpu.get_barrier_semaphore()

    def greet(step, carry):
        pl.semaphore_signal(
            barrier, inc=1, device_id=of_member(lax.rem(member + step, MEMBERS)), device_id_type=MESH
        )
        return carry

    lax.fori_loop(1, MEMBERS, greet, 0)

    def greet_far(step, carry):
        xx, zz = lax.div(step, 8), lax.rem(z + step, 8)

        @pl.when(jnp.logical_not(jnp.logical_and(jnp.logical_and(xx == x_high, zz == z), selfish)))
        def _():
            pl.semaphore_signal(barrier, inc=1, device_id=at_site(xx, zz, x_high), device_id_type=MESH)

        return carry

    lax.fori_loop(0, 16, greet_far, 0)
    slot_copy.wait()
    places = iota((FEEDS // LANES, LANES), 0) * LANES + iota((FEEDS // LANES, LANES), 1)
    found = [jnp.zeros((FEEDS // LANES, LANES), jnp.int32) for _ in range(4)]
    for feed in range(FEEDS):
        found[feed % 4] = jnp.where(places == slot[feed // LANES, feed % LANES], feed, found[feed % 4])
    owner_vmem[...] = jnp.maximum(jnp.maximum(found[0], found[1]), jnp.maximum(found[2], found[3]))
    owner_copy = pltpu.make_async_copy(owner_vmem, owner, owner_sem)
    owner_copy.start()

    for part in range(4):
        for piece in range(SPLIT // 4):
            volt_copies[part * (SPLIT // 4) + piece].wait()
        for block in range(8):
            flipped = jnp.transpose(volts[pl.ds(part * 256, 256), block * 256 : block * 256 + 256]).astype(jnp.float32)
            for half_rows in range(2):
                turned[pl.ds(block * 2048 + part * 2 + half_rows, 256, stride=8), :] = flipped[
                    :, half_rows * LANES : half_rows * LANES + LANES
                ]

    steer_copy.wait()
    steer = table[...].astype(jnp.bfloat16)
    owner_copy.wait()
    def gather(branch):
        for place in range(NS):
            at = branch * NS + place
            feed = owner[at // LANES, at % LANES]
            gridded[branch][pl.ds(place * 8, 8), :] = turned[pl.ds(feed * 8, 8), :]

    def transform(branch):
        data = [gridded[branch][pl.ds(q, NS, stride=8), :].astype(jnp.bfloat16) for q in range(8)]
        north[branch] = jnp.dot(steer, jnp.concatenate(data, axis=1), preferred_element_type=jnp.float32)

    first_row = iota((16, LANES), 0) == 0

    def energy(pol, strip):
        plus_rows, minus_rows = slice(strip * 16, strip * 16 + 16), slice(128 + strip * 16, 144 + strip * 16)
        for chunk in range(4):
            reals, imags = slice(chunk * LANES, chunk * LANES + LANES), slice(512 + chunk * LANES, 640 + chunk * LANES)
            at = pol * EW
            even = four_points(
                [north[at + e, plus_rows, reals] for e in range(EW)],
                [north[at + e, plus_rows, imags] for e in range(EW)],
            )
            odd = four_points(
                [north[at + e, minus_rows, reals] for e in range(EW)],
                [north[at + e, minus_rows, imags] for e in range(EW)],
            )
            for column in range(EW):
                (even_re, even_im), (odd_re, odd_im) = even[column], odd[column]
                plus_re, plus_im = even_re + odd_im, even_im - odd_re
                minus_re, minus_im = even_re - odd_im, even_im + odd_re
                if strip == 0:
                    plus_re, plus_im = jnp.where(first_row, even_re, plus_re), jnp.where(first_row, even_im, plus_im)
                    minus_re, minus_im = jnp.where(first_row, odd_re, minus_re), jnp.where(first_row, odd_im, minus_im)
                plus = plus_re * plus_re + plus_im * plus_im
                minus = minus_re * minus_re + minus_im * minus_im
                for first, part in ((strip * 32, plus), (strip * 32 + 16, minus)):
                    rows = slice(first, first + 16)
                    if pol == 0:
                        power[column, rows, reals] = part
                    else:
                        part = part + power[column, rows, reals]
                        high = part.astype(jnp.bfloat16)
                        highs[column, rows, reals] = high
                        rests[column, rows, reals] = (part - high.astype(jnp.float32)).astype(jnp.bfloat16)

    gather(0)
    for branch in range(POL * EW):
        if branch + 1 < POL * EW:
            gather(branch + 1)
        transform(branch)
        if branch >= EW:
            energy(0, 2 * (branch - EW))
            energy(0, 2 * (branch - EW) + 1)

    for strip in range(8):
        energy(1, strip)
    sample, place = iota((SAMPLES, LANES), 0), iota((SAMPLES, LANES), 1)
    chosen = (sample // CHANS == place % FRAMES) & (sample % CHANS // FSUM == place // FRAMES % BANDS)
    sums = jnp.zeros((NS, LANES), jnp.float32)
    for column in range(EW):
        own = chosen & (place // (BANDS * FRAMES) == column)
        adder = jnp.where(own, 0.5 / FEEDS, 0.0).astype(jnp.bfloat16)
        sums = sums + jnp.dot(highs[column], adder, preferred_element_type=jnp.float32)
        sums = sums + jnp.dot(rests[column], adder, preferred_element_type=jnp.float32)
    lane, source = iota((NS, NS), 1), iota((NS, NS), 0)
    output = lane // 8 % 16 * 16 + lane // 128 * 8 + lane % 8
    folded = jnp.where(output < 128, output, (256 - output) % 128)
    home = folded // 16 * 32 + folded % 16 + jnp.where(output < 128, 0, 16)
    order = jnp.where(source == home, 1.0, 0.0).astype(jnp.bfloat16)
    low_lanes = iota((16, LANES), 1) < LANES // 2
    binned = jnp.transpose(sums)
    high = binned.astype(jnp.bfloat16)
    rest = (binned - high.astype(jnp.float32)).astype(jnp.bfloat16)
    binned = jnp.dot(high, order, preferred_element_type=jnp.float32) + jnp.dot(
        rest, order, preferred_element_type=jnp.float32
    )
    for column in range(EW):
        for c in range(2):
            lanes = slice(c * LANES, c * LANES + LANES)
            one, two = binned[column * 32 : column * 32 + 16, lanes], binned[column * 32 + 16 : column * 32 + 32, lanes]
            target = (c * 2 + column // 2) * 4 + column % 2 * 2
            own_ref[target] = jnp.where(low_lanes, one, pltpu.roll(two, LANES // 2, 1))
            own_ref[target + 1] = jnp.where(low_lanes, pltpu.roll(one, LANES // 2, 1), two)

    pl.semaphore_wait(barrier, jnp.where(selfish, MEMBERS + 14, MEMBERS + 15))

    def near_copy(other):
        return pltpu.make_async_remote_copy(
            src_ref=own_ref.at[other],
            dst_ref=near.at[member],
            send_sem=near_send,
            recv_sem=near_recv,
            device_id=of_member(other),
            device_id_type=MESH,
        )

    for dy, dx, dc in itertools.product((2, 1, 3, 0), (1, 0), (1, 0)):
        if dy + dx + dc > 0:
            near_copy((lax.rem(core + dc, 2) * 2 + lax.rem(half + dx, 2)) * 4 + lax.rem(y + dy, 4)).start()
    mine = pltpu.make_async_copy(own_ref.at[member], near.at[member], self_sem)
    mine.start()
    mine.wait()
    pltpu.make_async_copy(near.at[0:15], near.at[0:15], near_recv).wait()

    shift_copy.wait()
    low_frames = iota((FRAMES, LANES), 1) < LANES // 2
    for c in range(2):
        for h in range(2):
            for pair in range(2):
                first = (c * 2 + h) * 4 + pair * 2
                for low in range(2):
                    one, two = near[first, low * 8 : low * 8 + 8, :], near[first + 1, low * 8 : low * 8 + 8, :]
                    frames = slice(h * 8, h * 8 + 8)
                    level_0[pair, c * 4 + low, frames, :] = jnp.where(low_frames, one, pltpu.roll(two, LANES // 2, 1))
                    level_0[pair, c * 4 + 2 + low, frames, :] = jnp.where(
                        low_frames, pltpu.roll(one, LANES // 2, 1), two
                    )

    buffers = (level_0, level_1, level_2)
    for level in range(LEVELS):
        span = 2**level
        current = buffers[level]
        for band in range(8):
            base, k = band - band % (2 * span), band % (2 * span)
            lower = base + k // 2
            lag = shift_ref[2 * span - 2 + k]
            for pair in range(2):
                total = current[pair, lower, 0:16, :] + current[pair, lower + span, pl.ds(lag, 16), :]
                if level < LEVELS - 1:
                    buffers[level + 1][pair, band, 0:16, :] = total
                else:
                    series[pair, pl.ds(band, 16, stride=8), :] = total
    low_half = iota((8, LANES), 1) < LANES // 2
    low_rows = iota((8, LANES), 0) < 4
    chunk = iota((8, LANES), 1) // 8
    ninth = [jnp.zeros((8, LANES), jnp.float32) for _ in range(8)]
    for pair in range(2):
        flipped = jnp.transpose(series[pair])
        for target in range(8):
            for low in range(2):
                tile = flipped[low * 64 + target * 8 : low * 64 + target * 8 + 8]
                at = pair * 2 + low
                crossed = pltpu.roll(pltpu.roll(tile, 4, 0), LANES // 2, 1)
                both = jnp.where(low_half == low_rows, tile, crossed)
                early[target, at * 4 : at * 4 + 4, :] = both[0:4]
                late[target, at * 4 : at * 4 + 4, :] = both[4:8]
                ninth[target] = jnp.where(chunk == at, pltpu.roll(tile, LANES // 2 + at * 8, 1), ninth[target])
    for target in range(8):
        early[target, 16:24, :] = ninth[target]

    source = x_high * 8 + z

    def to_early(target):
        return pltpu.make_async_remote_copy(
            src_ref=early.at[target],
            dst_ref=landed.at[source],
            send_sem=far_send.at[0],
            recv_sem=far_recv,
            device_id=at_site(half, target, 0),
            device_id_type=MESH,
        )

    def to_late(target):
        return pltpu.make_async_remote_copy(
            src_ref=late.at[target],
            dst_ref=landed.at[source, 0:16],
            send_sem=far_send.at[1],
            recv_sem=far_recv,
            device_id=at_site(half, target, 1),
            device_id_type=MESH,
        )

    early_self = jnp.logical_and(selfish, half == 0)
    late_self = jnp.logical_and(selfish, half == 1)
    for dz in (4, 3, 5, 2, 6, 1, 7):
        to_early(lax.rem(z + dz, 8)).start()
        to_late(lax.rem(z + dz, 8)).start()

    @pl.when(jnp.logical_not(early_self))
    def _():
        to_early(z).start()

    @pl.when(jnp.logical_not(late_self))
    def _():
        to_late(z).start()

    @pl.when(early_self)
    def _():
        copy = pltpu.make_async_copy(early.at[z], landed.at[source], self_sem)
        copy.start()
        copy.wait()

    @pl.when(late_self)
    def _():
        copy = pltpu.make_async_copy(late.at[z], landed.at[source, 0:16], self_sem)
        copy.start()
        copy.wait()

    def wait_for(part, sem):
        pltpu.make_async_copy(part, part, sem).wait()

    for h, rows in ((0, 24), (1, 16)):
        @pl.when(jnp.logical_and(half == h, selfish))
        def _():
            wait_for(landed.at[0:15, 0:rows], far_recv)

        @pl.when(jnp.logical_and(half == h, jnp.logical_not(selfish)))
        def _():
            wait_for(landed.at[:, 0:rows], far_recv)

    wait_for(own_ref.at[0:15], near_send)
    for flag, index, buffer in ((early_self, 0, early), (late_self, 1, late)):
        @pl.when(flag)
        def _():
            wait_for(buffer.at[0:7], far_send.at[index])

        @pl.when(jnp.logical_not(flag))
        def _():
            wait_for(buffer, far_send.at[index])


def finish_kernel(landed, out_ref, result, out_sem):
    chunk = iota((8, LANES), 1) // 8
    has_ninth = jnp.broadcast_to(lax.axis_index("tm"), (8, LANES)) == 0
    writes = []
    for xx in range(2):
        for pair in range(2):
            block = xx * 2 + pair
            tiles = []
            ninth = jnp.zeros((8, LANES), jnp.float32)
            for low in range(2):
                at = pair * 2 + low
                for zz in range(8):
                    tiles.append(landed[xx * 8 + zz, at * 4 : at * 4 + 8, :])
                    to = low * 8 + zz
                    ninth = jnp.where(
                        chunk == to, pltpu.roll(landed[xx * 8 + zz, 16:24, :], (to - at) * 8 % LANES, 1), ninth
                    )
            ninth = jnp.where(has_ninth, ninth, 0.0)
            tiles = swap_chunks(tiles)
            for high in range(2):
                for frame in range(8):
                    now = tiles[high * 8 + frame][0:4]
                    if frame < 7:
                        later = tiles[high * 8 + frame + 1][0:4]
                    else:
                        later = ninth[high * 4 : high * 4 + 4]
                    first = high * 64 + frame
                    result[block, pl.ds(first, 4, stride=16), :] = now * (1.0 / (FSUM * 8))
                    result[block, pl.ds(first + 8, 4, stride=16), :] = (now + later) * (1.0 / (FSUM * 16))
            write = pltpu.make_async_copy(
                result.at[block], out_ref.at[:, pl.ds(block * LANES, LANES)], out_sem.at[block]
            )
            write.start()
            writes.append(write)
    for write in writes:
        write.wait()


def finish(landed):
    return pl.pallas_call(
        finish_kernel,
        out_shape=pltpu.HBM((8 * BOXES * FRAMES, 512), jnp.float32),
        in_specs=[pl.BlockSpec(memory_space=pltpu.VMEM)],
        out_specs=pl.BlockSpec(memory_space=pltpu.HBM),
        scratch_shapes=[
            pltpu.VMEM((4, 128, LANES), jnp.float32),
            pltpu.SemaphoreType.DMA((4,)),
        ],
        compiler_params=pltpu.CompilerParams(vmem_limit_bytes=16 * 2**20),
        name="finish",
    )(landed)


def search(voltages, feed_slot, tree_shift):
    level = pltpu.VMEM((2, 8, 24, LANES), jnp.float32)
    dma = pltpu.SemaphoreType.DMA
    return pl.pallas_call(
        search_kernel,
        out_shape=pltpu.VMEM((16, 24, LANES), jnp.float32),
        in_specs=[pl.BlockSpec(memory_space=pltpu.HBM)] * 4,
        out_specs=pl.BlockSpec(memory_space=pltpu.VMEM),
        scratch_shapes=[
            pltpu.SMEM((FEEDS // LANES, LANES), jnp.int32),
            pltpu.VMEM((FEEDS // LANES, LANES), jnp.int32),
            pltpu.SMEM((FEEDS // LANES, LANES), jnp.int32),
            pltpu.SMEM((14,), jnp.int32),
            pltpu.VMEM((2 * SAMPLES, FEEDS), jnp.bfloat16),
            pltpu.VMEM((NS, NS), jnp.float32),
            pltpu.VMEM((FEEDS * 8, LANES), jnp.float32),
            [pltpu.VMEM((NS * 8, LANES), jnp.float32)] * (POL * EW),
            pltpu.VMEM((POL * EW, NS, 2 * SAMPLES), jnp.float32),
            pltpu.VMEM((EW, NS, SAMPLES), jnp.float32),
            pltpu.VMEM((EW, NS, SAMPLES), jnp.bfloat16),
            pltpu.VMEM((EW, NS, SAMPLES), jnp.bfloat16),
            pltpu.VMEM((MEMBERS, 16, LANES), jnp.float32),
            pltpu.VMEM((MEMBERS, 16, LANES), jnp.float32),
            level,
            level,
            level,
            pltpu.VMEM((2, 128, LANES), jnp.float32),
            pltpu.VMEM((8, 24, LANES), jnp.float32),
            pltpu.VMEM((8, 16, LANES), jnp.float32),
            dma,
            dma,
            dma,
            dma((SPLIT,)),
            dma,
            dma,
            dma,
            dma((2,)),
            dma,
            dma,
        ],
        compiler_params=pltpu.CompilerParams(
            collective_id=0, has_side_effects=True, vmem_limit_bytes=60 * 2**20
        ),
        name="search",
    )(
        feed_slot.reshape(FEEDS // LANES, LANES),
        tree_shift,
        voltages.reshape(2 * SAMPLES, FEEDS),
        steer_table(),
    )


def on_device(voltages, feed_slot, tree_shift):
    result = finish(search(voltages, feed_slot, tree_shift))
    return result.reshape(8, BOXES, FRAMES, 512)


def solution(mesh):
    placed = (P(None, "tm", "beam", None), P(), P())
    return jax.shard_map(
        on_device,
        mesh=mesh,
        in_specs=placed,
        out_specs=P("beam", None, "tm", None),
        check_vma=False,
    )
```

```python
import itertools
import math

import jax
import jax.numpy as jnp
import ml_dtypes
import numpy as np
from jax import lax
from jax.experimental import pallas as pl
from jax.experimental.pallas import tpu as pltpu
from jax.sharding import PartitionSpec as P

POL = 2
EW = 4
NS = 256
FEEDS = 2048
FSUM = 16
LEVELS = 3
BOXES = 2
FRAMES = 8
CHANS = 64
SAMPLES = FRAMES * CHANS
BANDS = CHANS // FSUM
MEMBERS = 16
SPLIT = 4
LANES = 128
MESH = pl.DeviceIdType.MESH


def steer_table():
    index = np.arange(NS)
    phase = (index[:, None] * index[None, :]) % NS
    angle = phase.astype(np.float32) * np.float32(2.0 * math.pi / NS)
    table = np.concatenate([np.cos(angle)[: NS // 2 + 1], np.sin(angle)[1 : NS // 2]], axis=0)
    return jnp.asarray(table.astype(ml_dtypes.bfloat16).astype(np.float32))


def contract_last(left, right):
    return lax.dot_general(left, right, (((1,), (1,)), ((), ())), preferred_element_type=jnp.float32)


def iota(shape, dim):
    return lax.broadcasted_iota(jnp.int32, shape, dim)


def four_points(re, im):
    even_re, even_im = re[0] + re[2], im[0] + im[2]
    odd_re, odd_im = re[0] - re[2], im[0] - im[2]
    side_re, side_im = re[1] + re[3], im[1] + im[3]
    diff_re, diff_im = re[1] - re[3], im[1] - im[3]
    return [
        (even_re + side_re, even_im + side_im),
        (odd_re + diff_im, odd_im - diff_re),
        (even_re - side_re, even_im - side_im),
        (odd_re - diff_im, odd_im + diff_re),
    ]


def swap_chunks(tiles):
    lane = lax.broadcasted_iota(jnp.int32, (8, LANES), 1)
    tiles = list(tiles)
    for bit in range(4):
        span = 8 << bit
        low_half = (lane // span) % 2 == 0
        for first in range(16):
            if first >> bit & 1:
                continue
            second = first | 1 << bit
            one, two = tiles[first], tiles[second]
            tiles[first] = jnp.where(low_half, one, pltpu.roll(two, span, 1))
            tiles[second] = jnp.where(low_half, pltpu.roll(one, LANES - span, 1), two)
    return tiles


def search_kernel(
    slot_hbm, shift_hbm, volt_hbm, table_hbm, landed,
    slot, owner_vmem, owner, shift_ref, volts, table, turned, gridded, north, power, highs, rests,
    own_ref, near, level_0, level_1, level_2, series, early, late,
    slot_sem, owner_sem, shift_sem, volt_sem, steer_sem,
    near_send, near_recv, far_send, far_recv, self_sem,
):
    slot_copy = pltpu.make_async_copy(slot_hbm, slot, slot_sem)
    steer_copy = pltpu.make_async_copy(table_hbm, table, steer_sem)
    shift_copy = pltpu.make_async_copy(shift_hbm, shift_ref, shift_sem)
    volt_copies = [
        pltpu.make_async_copy(
            volt_hbm.at[pl.ds(part * 1024 // SPLIT, 1024 // SPLIT)],
            volts.at[pl.ds(part * 1024 // SPLIT, 1024 // SPLIT)],
            volt_sem.at[part],
        )
        for part in range(SPLIT)
    ]
    for copy in [slot_copy] + volt_copies + [steer_copy, shift_copy]:
        copy.start()

    for buffer in (level_0, level_1, level_2):
        buffer[:, :, 16:24, :] = jnp.zeros((2, 8, 8, LANES), jnp.float32)
    place = lax.axis_index("beam")
    half = lax.axis_index("tm")
    core = lax.rem(place, 2)
    site = lax.div(place, 2)
    z = lax.rem(site, 8)
    y = lax.rem(lax.div(site, 8), 4)
    x_high = lax.div(site, 32)
    member = (core * 2 + half) * 4 + y
    selfish = x_high == half

    def of_member(other):
        c, h, at = lax.div(other, 8), lax.rem(lax.div(other, 4), 2), lax.rem(other, 4)
        return (((x_high * 4 + at) * 8 + z) * 2 + c, h)

    def at_site(xx, zz, h):
        return (((xx * 4 + y) * 8 + zz) * 2 + core, h)

    barrier = pltpu.get_barrier_semaphore()

    def greet(step, carry):
        pl.semaphore_signal(
            barrier, inc=1, device_id=of_member(lax.rem(member + step, MEMBERS)), device_id_type=MESH
        )
        return carry

    lax.fori_loop(1, MEMBERS, greet, 0)

    def greet_far(step, carry):
        xx, zz = lax.div(step, 8), lax.rem(z + step, 8)

        @pl.when(jnp.logical_not(jnp.logical_and(jnp.logical_and(xx == x_high, zz == z), selfish)))
        def _():
            pl.semaphore_signal(barrier, inc=1, device_id=at_site(xx, zz, x_high), device_id_type=MESH)

        return carry

    lax.fori_loop(0, 16, greet_far, 0)
    slot_copy.wait()
    places = iota((FEEDS // LANES, LANES), 0) * LANES + iota((FEEDS // LANES, LANES), 1)
    found = [jnp.zeros((FEEDS // LANES, LANES), jnp.int32) for _ in range(4)]
    for feed in range(FEEDS):
        found[feed % 4] = jnp.where(places == slot[feed // LANES, feed % LANES], feed, found[feed % 4])
    owner_vmem[...] = jnp.maximum(jnp.maximum(found[0], found[1]), jnp.maximum(found[2], found[3]))
    owner_copy = pltpu.make_async_copy(owner_vmem, owner, owner_sem)
    owner_copy.start()

    for part in range(4):
        for piece in range(SPLIT // 4):
            volt_copies[part * (SPLIT // 4) + piece].wait()
        for block in range(8):
            flipped = jnp.transpose(volts[pl.ds(part * 256, 256), block * 256 : block * 256 + 256]).astype(jnp.float32)
            for half_rows in range(2):
                turned[pl.ds(block * 2048 + part * 2 + half_rows, 256, stride=8), :] = flipped[
                    :, half_rows * LANES : half_rows * LANES + LANES
                ]

    steer_copy.wait()
    steer = table[...].astype(jnp.bfloat16)
    owner_copy.wait()
    def gather(branch):
        for place in range(NS):
            at = branch * NS + place
            feed = owner[at // LANES, at % LANES]
            gridded[branch][pl.ds(place * 8, 8), :] = turned[pl.ds(feed * 8, 8), :]

    def transform(branch):
        data = [gridded[branch][pl.ds(q, NS, stride=8), :].astype(jnp.bfloat16) for q in range(8)]
        north[branch] = jnp.dot(steer, jnp.concatenate(data, axis=1), preferred_element_type=jnp.float32)

    first_row = iota((16, 256), 0) == 0

    def energy(pol, strip):
        plus_rows, minus_rows = slice(strip * 16, strip * 16 + 16), slice(128 + strip * 16, 144 + strip * 16)
        for chunk in range(2):
            reals, imags = slice(chunk * 256, chunk * 256 + 256), slice(512 + chunk * 256, 768 + chunk * 256)
            at = pol * EW
            even = four_points(
                [north[at + e, plus_rows, reals] for e in range(EW)],
                [north[at + e, plus_rows, imags] for e in range(EW)],
            )
            odd = four_points(
                [north[at + e, minus_rows, reals] for e in range(EW)],
                [north[at + e, minus_rows, imags] for e in range(EW)],
            )
            for column in range(EW):
                (even_re, even_im), (odd_re, odd_im) = even[column], odd[column]
                plus_re, plus_im = even_re + odd_im, even_im - odd_re
                minus_re, minus_im = even_re - odd_im, even_im + odd_re
                if strip == 0:
                    plus_re, plus_im = jnp.where(first_row, even_re, plus_re), jnp.where(first_row, even_im, plus_im)
                    minus_re, minus_im = jnp.where(first_row, odd_re, minus_re), jnp.where(first_row, odd_im, minus_im)
                plus = plus_re * plus_re + plus_im * plus_im
                minus = minus_re * minus_re + minus_im * minus_im
                for first, part in ((strip * 32, plus), (strip * 32 + 16, minus)):
                    rows = slice(first, first + 16)
                    if pol == 0:
                        power[column, rows, reals] = part
                    else:
                        part = part + power[column, rows, reals]
                        high = part.astype(jnp.bfloat16)
                        highs[column, rows, reals] = high
                        rests[column, rows, reals] = (part - high.astype(jnp.float32)).astype(jnp.bfloat16)

    gather(0)
    for branch in range(POL * EW):
        if branch + 1 < POL * EW:
            gather(branch + 1)
        transform(branch)

    for strip in range(8):
        energy(0, strip)
        energy(1, strip)
    sample, place = iota((SAMPLES, LANES), 0), iota((SAMPLES, LANES), 1)
    chosen = (sample // CHANS == place % FRAMES) & (sample % CHANS // FSUM == place // FRAMES % BANDS)
    sums = jnp.zeros((NS, LANES), jnp.float32)
    for column in range(EW):
        own = chosen & (place // (BANDS * FRAMES) == column)
        adder = jnp.where(own, 0.5 / FEEDS, 0.0).astype(jnp.bfloat16)
        sums = sums + jnp.dot(highs[column], adder, preferred_element_type=jnp.float32)
        sums = sums + jnp.dot(rests[column], adder, preferred_element_type=jnp.float32)
    lane, source = iota((NS, NS), 1), iota((NS, NS), 0)
    output = lane // 8 % 16 * 16 + lane // 128 * 8 + lane % 8
    folded = jnp.where(output < 128, output, (256 - output) % 128)
    home = folded // 16 * 32 + folded % 16 + jnp.where(output < 128, 0, 16)
    order = jnp.where(source == home, 1.0, 0.0).astype(jnp.bfloat16)
    low_lanes = iota((16, LANES), 1) < LANES // 2
    binned = jnp.transpose(sums)
    high = binned.astype(jnp.bfloat16)
    rest = (binned - high.astype(jnp.float32)).astype(jnp.bfloat16)
    binned = jnp.dot(high, order, preferred_element_type=jnp.float32) + jnp.dot(
        rest, order, preferred_element_type=jnp.float32
    )
    for column in range(EW):
        for c in range(2):
            lanes = slice(c * LANES, c * LANES + LANES)
            one, two = binned[column * 32 : column * 32 + 16, lanes], binned[column * 32 + 16 : column * 32 + 32, lanes]
            target = (c * 2 + column // 2) * 4 + column % 2 * 2
            own_ref[target] = jnp.where(low_lanes, one, pltpu.roll(two, LANES // 2, 1))
            own_ref[target + 1] = jnp.where(low_lanes, pltpu.roll(one, LANES // 2, 1), two)

    pl.semaphore_wait(barrier, jnp.where(selfish, MEMBERS + 14, MEMBERS + 15))

    def near_copy(other):
        return pltpu.make_async_remote_copy(
            src_ref=own_ref.at[other],
            dst_ref=near.at[member],
            send_sem=near_send,
            recv_sem=near_recv,
            device_id=of_member(other),
            device_id_type=MESH,
        )

    for dy, dx, dc in itertools.product((2, 1, 3, 0), (1, 0), (1, 0)):
        if dy + dx + dc > 0:
            near_copy((lax.rem(core + dc, 2) * 2 + lax.rem(half + dx, 2)) * 4 + lax.rem(y + dy, 4)).start()
    mine = pltpu.make_async_copy(own_ref.at[member], near.at[member], self_sem)
    mine.start()
    mine.wait()
    pltpu.make_async_copy(near.at[0:15], near.at[0:15], near_recv).wait()

    shift_copy.wait()
    low_frames = iota((FRAMES, LANES), 1) < LANES // 2
    for c in range(2):
        for h in range(2):
            for pair in range(2):
                first = (c * 2 + h) * 4 + pair * 2
                for low in range(2):
                    one, two = near[first, low * 8 : low * 8 + 8, :], near[first + 1, low * 8 : low * 8 + 8, :]
                    frames = slice(h * 8, h * 8 + 8)
                    level_0[pair, c * 4 + low, frames, :] = jnp.where(low_frames, one, pltpu.roll(two, LANES // 2, 1))
                    level_0[pair, c * 4 + 2 + low, frames, :] = jnp.where(
                        low_frames, pltpu.roll(one, LANES // 2, 1), two
                    )

    buffers = (level_0, level_1, level_2)
    for level in range(LEVELS):
        span = 2**level
        current = buffers[level]
        for band in range(8):
            base, k = band - band % (2 * span), band % (2 * span)
            lower = base + k // 2
            lag = shift_ref[2 * span - 2 + k]
            for pair in range(2):
                total = current[pair, lower, 0:16, :] + current[pair, lower + span, pl.ds(lag, 16), :]
                if level < LEVELS - 1:
                    buffers[level + 1][pair, band, 0:16, :] = total
                else:
                    series[pair, pl.ds(band, 16, stride=8), :] = total
    low_half = iota((8, LANES), 1) < LANES // 2
    low_rows = iota((8, LANES), 0) < 4
    chunk = iota((8, LANES), 1) // 8
    ninth = [jnp.zeros((8, LANES), jnp.float32) for _ in range(8)]
    for pair in range(2):
        flipped = jnp.transpose(series[pair])
        for target in range(8):
            for low in range(2):
                tile = flipped[low * 64 + target * 8 : low * 64 + target * 8 + 8]
                at = pair * 2 + low
                crossed = pltpu.roll(pltpu.roll(tile, 4, 0), LANES // 2, 1)
                both = jnp.where(low_half == low_rows, tile, crossed)
                early[target, at * 4 : at * 4 + 4, :] = both[0:4]
                late[target, at * 4 : at * 4 + 4, :] = both[4:8]
                ninth[target] = jnp.where(chunk == at, pltpu.roll(tile, LANES // 2 + at * 8, 1), ninth[target])
    for target in range(8):
        early[target, 16:24, :] = ninth[target]

    source = x_high * 8 + z

    def to_early(target):
        return pltpu.make_async_remote_copy(
            src_ref=early.at[target],
            dst_ref=landed.at[source],
            send_sem=far_send.at[0],
            recv_sem=far_recv,
            device_id=at_site(half, target, 0),
            device_id_type=MESH,
        )

    def to_late(target):
        return pltpu.make_async_remote_copy(
            src_ref=late.at[target],
            dst_ref=landed.at[source, 0:16],
            send_sem=far_send.at[1],
            recv_sem=far_recv,
            device_id=at_site(half, target, 1),
            device_id_type=MESH,
        )

    early_self = jnp.logical_and(selfish, half == 0)
    late_self = jnp.logical_and(selfish, half == 1)
    for dz in (4, 3, 5, 2, 6, 1, 7):
        to_early(lax.rem(z + dz, 8)).start()
        to_late(lax.rem(z + dz, 8)).start()

    @pl.when(jnp.logical_not(early_self))
    def _():
        to_early(z).start()

    @pl.when(jnp.logical_not(late_self))
    def _():
        to_late(z).start()

    @pl.when(early_self)
    def _():
        copy = pltpu.make_async_copy(early.at[z], landed.at[source], self_sem)
        copy.start()
        copy.wait()

    @pl.when(late_self)
    def _():
        copy = pltpu.make_async_copy(late.at[z], landed.at[source, 0:16], self_sem)
        copy.start()
        copy.wait()

    def wait_for(part, sem):
        pltpu.make_async_copy(part, part, sem).wait()

    for h, rows in ((0, 24), (1, 16)):
        @pl.when(jnp.logical_and(half == h, selfish))
        def _():
            wait_for(landed.at[0:15, 0:rows], far_recv)

        @pl.when(jnp.logical_and(half == h, jnp.logical_not(selfish)))
        def _():
            wait_for(landed.at[:, 0:rows], far_recv)

    wait_for(own_ref.at[0:15], near_send)
    for flag, index, buffer in ((early_self, 0, early), (late_self, 1, late)):
        @pl.when(flag)
        def _():
            wait_for(buffer.at[0:7], far_send.at[index])

        @pl.when(jnp.logical_not(flag))
        def _():
            wait_for(buffer, far_send.at[index])


def finish_kernel(landed, out_ref, result, out_sem):
    chunk = iota((8, LANES), 1) // 8
    has_ninth = jnp.broadcast_to(lax.axis_index("tm"), (8, LANES)) == 0
    writes = []
    for xx in range(2):
        for pair in range(2):
            block = xx * 2 + pair
            tiles = []
            ninth = jnp.zeros((8, LANES), jnp.float32)
            for low in range(2):
                at = pair * 2 + low
                for zz in range(8):
                    tiles.append(landed[xx * 8 + zz, at * 4 : at * 4 + 8, :])
                    to = low * 8 + zz
                    ninth = jnp.where(
                        chunk == to, pltpu.roll(landed[xx * 8 + zz, 16:24, :], (to - at) * 8 % LANES, 1), ninth
                    )
            ninth = jnp.where(has_ninth, ninth, 0.0)
            tiles = swap_chunks(tiles)
            for high in range(2):
                for frame in range(8):
                    now = tiles[high * 8 + frame][0:4]
                    if frame < 7:
                        later = tiles[high * 8 + frame + 1][0:4]
                    else:
                        later = ninth[high * 4 : high * 4 + 4]
                    first = high * 64 + frame
                    result[block, pl.ds(first, 4, stride=16), :] = now * (1.0 / (FSUM * 8))
                    result[block, pl.ds(first + 8, 4, stride=16), :] = (now + later) * (1.0 / (FSUM * 16))
            write = pltpu.make_async_copy(
                result.at[block], out_ref.at[:, pl.ds(block * LANES, LANES)], out_sem.at[block]
            )
            write.start()
            writes.append(write)
    for write in writes:
        write.wait()


def finish(landed):
    return pl.pallas_call(
        finish_kernel,
        out_shape=pltpu.HBM((8 * BOXES * FRAMES, 512), jnp.float32),
        in_specs=[pl.BlockSpec(memory_space=pltpu.VMEM)],
        out_specs=pl.BlockSpec(memory_space=pltpu.HBM),
        scratch_shapes=[
            pltpu.VMEM((4, 128, LANES), jnp.float32),
            pltpu.SemaphoreType.DMA((4,)),
        ],
        compiler_params=pltpu.CompilerParams(vmem_limit_bytes=16 * 2**20),
        name="finish",
    )(landed)


def search(voltages, feed_slot, tree_shift):
    level = pltpu.VMEM((2, 8, 24, LANES), jnp.float32)
    dma = pltpu.SemaphoreType.DMA
    return pl.pallas_call(
        search_kernel,
        out_shape=pltpu.VMEM((16, 24, LANES), jnp.float32),
        in_specs=[pl.BlockSpec(memory_space=pltpu.HBM)] * 4,
        out_specs=pl.BlockSpec(memory_space=pltpu.VMEM),
        scratch_shapes=[
            pltpu.SMEM((FEEDS // LANES, LANES), jnp.int32),
            pltpu.VMEM((FEEDS // LANES, LANES), jnp.int32),
            pltpu.SMEM((FEEDS // LANES, LANES), jnp.int32),
            pltpu.SMEM((14,), jnp.int32),
            pltpu.VMEM((2 * SAMPLES, FEEDS), jnp.bfloat16),
            pltpu.VMEM((NS, NS), jnp.float32),
            pltpu.VMEM((FEEDS * 8, LANES), jnp.float32),
            [pltpu.VMEM((NS * 8, LANES), jnp.float32)] * (POL * EW),
            pltpu.VMEM((POL * EW, NS, 2 * SAMPLES), jnp.float32),
            pltpu.VMEM((EW, NS, SAMPLES), jnp.float32),
            pltpu.VMEM((EW, NS, SAMPLES), jnp.bfloat16),
            pltpu.VMEM((EW, NS, SAMPLES), jnp.bfloat16),
            pltpu.VMEM((MEMBERS, 16, LANES), jnp.float32),
            pltpu.VMEM((MEMBERS, 16, LANES), jnp.float32),
            level,
            level,
            level,
            pltpu.VMEM((2, 128, LANES), jnp.float32),
            pltpu.VMEM((8, 24, LANES), jnp.float32),
            pltpu.VMEM((8, 16, LANES), jnp.float32),
            dma,
            dma,
            dma,
            dma((SPLIT,)),
            dma,
            dma,
            dma,
            dma((2,)),
            dma,
            dma,
        ],
        compiler_params=pltpu.CompilerParams(
            collective_id=0, has_side_effects=True, vmem_limit_bytes=60 * 2**20
        ),
        name="search",
    )(
        feed_slot.reshape(FEEDS // LANES, LANES),
        tree_shift,
        voltages.reshape(2 * SAMPLES, FEEDS),
        steer_table(),
    )


def on_device(voltages, feed_slot, tree_shift):
    result = finish(search(voltages, feed_slot, tree_shift))
    return result.reshape(8, BOXES, FRAMES, 512)


def solution(mesh):
    placed = (P(None, "tm", "beam", None), P(), P())
    return jax.shard_map(
        on_device,
        mesh=mesh,
        in_specs=placed,
        out_specs=P("beam", None, "tm", None),
        check_vma=False,
    )
```

```python
import itertools
import math

import jax
import jax.numpy as jnp
import ml_dtypes
import numpy as np
from jax import lax
from jax.experimental import pallas as pl
from jax.experimental.pallas import tpu as pltpu
from jax.sharding import PartitionSpec as P

POL = 2
EW = 4
NS = 256
FEEDS = 2048
FSUM = 16
LEVELS = 3
BOXES = 2
FRAMES = 8
CHANS = 64
SAMPLES = FRAMES * CHANS
BANDS = CHANS // FSUM
MEMBERS = 16
SPLIT = 4
LANES = 128
MESH = pl.DeviceIdType.MESH


def steer_table():
    index = np.arange(NS)
    phase = (index[:, None] * index[None, :]) % NS
    angle = phase.astype(np.float32) * np.float32(2.0 * math.pi / NS)
    table = np.concatenate([np.cos(angle)[: NS // 2 + 1], np.sin(angle)[1 : NS // 2]], axis=0)
    return jnp.asarray(table.astype(ml_dtypes.bfloat16).astype(np.float32))


def contract_last(left, right):
    return lax.dot_general(left, right, (((1,), (1,)), ((), ())), preferred_element_type=jnp.float32)


def iota(shape, dim):
    return lax.broadcasted_iota(jnp.int32, shape, dim)


def four_points(re, im):
    even_re, even_im = re[0] + re[2], im[0] + im[2]
    odd_re, odd_im = re[0] - re[2], im[0] - im[2]
    side_re, side_im = re[1] + re[3], im[1] + im[3]
    diff_re, diff_im = re[1] - re[3], im[1] - im[3]
    return [
        (even_re + side_re, even_im + side_im),
        (odd_re + diff_im, odd_im - diff_re),
        (even_re - side_re, even_im - side_im),
        (odd_re - diff_im, odd_im + diff_re),
    ]


def swap_chunks(tiles):
    lane = lax.broadcasted_iota(jnp.int32, (8, LANES), 1)
    tiles = list(tiles)
    for bit in range(4):
        span = 8 << bit
        low_half = (lane // span) % 2 == 0
        for first in range(16):
            if first >> bit & 1:
                continue
            second = first | 1 << bit
            one, two = tiles[first], tiles[second]
            tiles[first] = jnp.where(low_half, one, pltpu.roll(two, span, 1))
            tiles[second] = jnp.where(low_half, pltpu.roll(one, LANES - span, 1), two)
    return tiles


def search_kernel(
    slot_hbm, shift_hbm, volt_hbm, table_hbm, landed,
    slot, owner_vmem, owner, shift_ref, volts, table, turned, gridded, north, power, highs, rests,
    own_ref, near, level_0, level_1, level_2, series, early, late,
    slot_sem, owner_sem, shift_sem, volt_sem, steer_sem,
    near_send, near_recv, far_send, far_recv, self_sem,
):
    slot_copy = pltpu.make_async_copy(slot_hbm, slot, slot_sem)
    steer_copy = pltpu.make_async_copy(table_hbm, table, steer_sem)
    shift_copy = pltpu.make_async_copy(shift_hbm, shift_ref, shift_sem)
    volt_copies = [
        pltpu.make_async_copy(
            volt_hbm.at[pl.ds(part * 1024 // SPLIT, 1024 // SPLIT)],
            volts.at[pl.ds(part * 1024 // SPLIT, 1024 // SPLIT)],
            volt_sem.at[part],
        )
        for part in range(SPLIT)
    ]
    for copy in [slot_copy] + volt_copies + [steer_copy, shift_copy]:
        copy.start()

    for buffer in (level_0, level_1, level_2):
        buffer[:, :, 16:24, :] = jnp.zeros((2, 8, 8, LANES), jnp.float32)
    place = lax.axis_index("beam")
    half = lax.axis_index("tm")
    core = lax.rem(place, 2)
    site = lax.div(place, 2)
    z = lax.rem(site, 8)
    y = lax.rem(lax.div(site, 8), 4)
    x_high = lax.div(site, 32)
    member = (core * 2 + half) * 4 + y
    selfish = x_high == half

    def of_member(other):
        c, h, at = lax.div(other, 8), lax.rem(lax.div(other, 4), 2), lax.rem(other, 4)
        return (((x_high * 4 + at) * 8 + z) * 2 + c, h)

    def at_site(xx, zz, h):
        return (((xx * 4 + y) * 8 + zz) * 2 + core, h)

    barrier = pltpu.get_barrier_semaphore()

    def greet(step, carry):
        pl.semaphore_signal(
            barrier, inc=1, device_id=of_member(lax.rem(member + step, MEMBERS)), device_id_type=MESH
        )
        return carry

    lax.fori_loop(1, MEMBERS, greet, 0)

    def greet_far(step, carry):
        xx, zz = lax.div(step, 8), lax.rem(z + step, 8)

        @pl.when(jnp.logical_not(jnp.logical_and(jnp.logical_and(xx == x_high, zz == z), selfish)))
        def _():
            pl.semaphore_signal(barrier, inc=1, device_id=at_site(xx, zz, x_high), device_id_type=MESH)

        return carry

    lax.fori_loop(0, 16, greet_far, 0)
    slot_copy.wait()
    places = iota((FEEDS // LANES, LANES), 0) * LANES + iota((FEEDS // LANES, LANES), 1)
    found = [jnp.zeros((FEEDS // LANES, LANES), jnp.int32) for _ in range(4)]
    for feed in range(FEEDS):
        found[feed % 4] = jnp.where(places == slot[feed // LANES, feed % LANES], feed, found[feed % 4])
    owner_vmem[...] = jnp.maximum(jnp.maximum(found[0], found[1]), jnp.maximum(found[2], found[3]))
    owner_copy = pltpu.make_async_copy(owner_vmem, owner, owner_sem)
    owner_copy.start()

    for part in range(4):
        for piece in range(SPLIT // 4):
            volt_copies[part * (SPLIT // 4) + piece].wait()
        for block in range(8):
            flipped = jnp.transpose(volts[pl.ds(part * 256, 256), block * 256 : block * 256 + 256]).astype(jnp.float32)
            for half_rows in range(2):
                turned[pl.ds(block * 2048 + part * 2 + half_rows, 256, stride=8), :] = flipped[
                    :, half_rows * LANES : half_rows * LANES + LANES
                ]

    steer_copy.wait()
    steer = table[...].astype(jnp.bfloat16)
    owner_copy.wait()
    def gather(branch):
        for place in range(NS):
            at = branch * NS + place
            feed = owner[at // LANES, at % LANES]
            gridded[branch][pl.ds(place * 8, 8), :] = turned[pl.ds(feed * 8, 8), :]

    def transform(branch):
        data = [gridded[branch][pl.ds(q, NS, stride=8), :].astype(jnp.bfloat16) for q in range(8)]
        north[branch] = jnp.dot(steer, jnp.concatenate(data, axis=1), preferred_element_type=jnp.float32)

    first_row = iota((16, SAMPLES), 0) == 0

    def energy(pol, strip):
        plus_rows, minus_rows = slice(strip * 16, strip * 16 + 16), slice(128 + strip * 16, 144 + strip * 16)
        for chunk in range(1):
            reals, imags = slice(0, SAMPLES), slice(SAMPLES, 2 * SAMPLES)
            at = pol * EW
            even = four_points(
                [north[at + e, plus_rows, reals] for e in range(EW)],
                [north[at + e, plus_rows, imags] for e in range(EW)],
            )
            odd = four_points(
                [north[at + e, minus_rows, reals] for e in range(EW)],
                [north[at + e, minus_rows, imags] for e in range(EW)],
            )
            for column in range(EW):
                (even_re, even_im), (odd_re, odd_im) = even[column], odd[column]
                plus_re, plus_im = even_re + odd_im, even_im - odd_re
                minus_re, minus_im = even_re - odd_im, even_im + odd_re
                if strip == 0:
                    plus_re, plus_im = jnp.where(first_row, even_re, plus_re), jnp.where(first_row, even_im, plus_im)
                    minus_re, minus_im = jnp.where(first_row, odd_re, minus_re), jnp.where(first_row, odd_im, minus_im)
                plus = plus_re * plus_re + plus_im * plus_im
                minus = minus_re * minus_re + minus_im * minus_im
                for first, part in ((strip * 32, plus), (strip * 32 + 16, minus)):
                    rows = slice(first, first + 16)
                    if pol == 0:
                        power[column, rows, reals] = part
                    else:
                        part = part + power[column, rows, reals]
                        high = part.astype(jnp.bfloat16)
                        highs[column, rows, reals] = high
                        rests[column, rows, reals] = (part - high.astype(jnp.float32)).astype(jnp.bfloat16)

    gather(0)
    for branch in range(POL * EW):
        if branch + 1 < POL * EW:
            gather(branch + 1)
        transform(branch)

    for strip in range(8):
        energy(0, strip)
        energy(1, strip)
    sample, place = iota((SAMPLES, LANES), 0), iota((SAMPLES, LANES), 1)
    chosen = (sample // CHANS == place % FRAMES) & (sample % CHANS // FSUM == place // FRAMES % BANDS)
    sums = jnp.zeros((NS, LANES), jnp.float32)
    for column in range(EW):
        own = chosen & (place // (BANDS * FRAMES) == column)
        adder = jnp.where(own, 0.5 / FEEDS, 0.0).astype(jnp.bfloat16)
        sums = sums + jnp.dot(highs[column], adder, preferred_element_type=jnp.float32)
        sums = sums + jnp.dot(rests[column], adder, preferred_element_type=jnp.float32)
    lane, source = iota((NS, NS), 1), iota((NS, NS), 0)
    output = lane // 8 % 16 * 16 + lane // 128 * 8 + lane % 8
    folded = jnp.where(output < 128, output, (256 - output) % 128)
    home = folded // 16 * 32 + folded % 16 + jnp.where(output < 128, 0, 16)
    order = jnp.where(source == home, 1.0, 0.0).astype(jnp.bfloat16)
    low_lanes = iota((16, LANES), 1) < LANES // 2
    binned = jnp.transpose(sums)
    high = binned.astype(jnp.bfloat16)
    rest = (binned - high.astype(jnp.float32)).astype(jnp.bfloat16)
    binned = jnp.dot(high, order, preferred_element_type=jnp.float32) + jnp.dot(
        rest, order, preferred_element_type=jnp.float32
    )
    for column in range(EW):
        for c in range(2):
            lanes = slice(c * LANES, c * LANES + LANES)
            one, two = binned[column * 32 : column * 32 + 16, lanes], binned[column * 32 + 16 : column * 32 + 32, lanes]
            target = (c * 2 + column // 2) * 4 + column % 2 * 2
            own_ref[target] = jnp.where(low_lanes, one, pltpu.roll(two, LANES // 2, 1))
            own_ref[target + 1] = jnp.where(low_lanes, pltpu.roll(one, LANES // 2, 1), two)

    pl.semaphore_wait(barrier, jnp.where(selfish, MEMBERS + 14, MEMBERS + 15))

    def near_copy(other):
        return pltpu.make_async_remote_copy(
            src_ref=own_ref.at[other],
            dst_ref=near.at[member],
            send_sem=near_send,
            recv_sem=near_recv,
            device_id=of_member(other),
            device_id_type=MESH,
        )

    for dy, dx, dc in itertools.product((2, 1, 3, 0), (1, 0), (1, 0)):
        if dy + dx + dc > 0:
            near_copy((lax.rem(core + dc, 2) * 2 + lax.rem(half + dx, 2)) * 4 + lax.rem(y + dy, 4)).start()
    mine = pltpu.make_async_copy(own_ref.at[member], near.at[member], self_sem)
    mine.start()
    mine.wait()
    pltpu.make_async_copy(near.at[0:15], near.at[0:15], near_recv).wait()

    shift_copy.wait()
    low_frames = iota((FRAMES, LANES), 1) < LANES // 2
    for c in range(2):
        for h in range(2):
            for pair in range(2):
                first = (c * 2 + h) * 4 + pair * 2
                for low in range(2):
                    one, two = near[first, low * 8 : low * 8 + 8, :], near[first + 1, low * 8 : low * 8 + 8, :]
                    frames = slice(h * 8, h * 8 + 8)
                    level_0[pair, c * 4 + low, frames, :] = jnp.where(low_frames, one, pltpu.roll(two, LANES // 2, 1))
                    level_0[pair, c * 4 + 2 + low, frames, :] = jnp.where(
                        low_frames, pltpu.roll(one, LANES // 2, 1), two
                    )

    buffers = (level_0, level_1, level_2)
    for level in range(LEVELS):
        span = 2**level
        current = buffers[level]
        for band in range(8):
            base, k = band - band % (2 * span), band % (2 * span)
            lower = base + k // 2
            lag = shift_ref[2 * span - 2 + k]
            for pair in range(2):
                total = current[pair, lower, 0:16, :] + current[pair, lower + span, pl.ds(lag, 16), :]
                if level < LEVELS - 1:
                    buffers[level + 1][pair, band, 0:16, :] = total
                else:
                    series[pair, pl.ds(band, 16, stride=8), :] = total
    low_half = iota((8, LANES), 1) < LANES // 2
    low_rows = iota((8, LANES), 0) < 4
    chunk = iota((8, LANES), 1) // 8
    ninth = [jnp.zeros((8, LANES), jnp.float32) for _ in range(8)]
    for pair in range(2):
        flipped = jnp.transpose(series[pair])
        for target in range(8):
            for low in range(2):
                tile = flipped[low * 64 + target * 8 : low * 64 + target * 8 + 8]
                at = pair * 2 + low
                crossed = pltpu.roll(pltpu.roll(tile, 4, 0), LANES // 2, 1)
                both = jnp.where(low_half == low_rows, tile, crossed)
                early[target, at * 4 : at * 4 + 4, :] = both[0:4]
                late[target, at * 4 : at * 4 + 4, :] = both[4:8]
                ninth[target] = jnp.where(chunk == at, pltpu.roll(tile, LANES // 2 + at * 8, 1), ninth[target])
    for target in range(8):
        early[target, 16:24, :] = ninth[target]

    source = x_high * 8 + z

    def to_early(target):
        return pltpu.make_async_remote_copy(
            src_ref=early.at[target],
            dst_ref=landed.at[source],
            send_sem=far_send.at[0],
            recv_sem=far_recv,
            device_id=at_site(half, target, 0),
            device_id_type=MESH,
        )

    def to_late(target):
        return pltpu.make_async_remote_copy(
            src_ref=late.at[target],
            dst_ref=landed.at[source, 0:16],
            send_sem=far_send.at[1],
            recv_sem=far_recv,
            device_id=at_site(half, target, 1),
            device_id_type=MESH,
        )

    early_self = jnp.logical_and(selfish, half == 0)
    late_self = jnp.logical_and(selfish, half == 1)
    for dz in (4, 3, 5, 2, 6, 1, 7):
        to_early(lax.rem(z + dz, 8)).start()
        to_late(lax.rem(z + dz, 8)).start()

    @pl.when(jnp.logical_not(early_self))
    def _():
        to_early(z).start()

    @pl.when(jnp.logical_not(late_self))
    def _():
        to_late(z).start()

    @pl.when(early_self)
    def _():
        copy = pltpu.make_async_copy(early.at[z], landed.at[source], self_sem)
        copy.start()
        copy.wait()

    @pl.when(late_self)
    def _():
        copy = pltpu.make_async_copy(late.at[z], landed.at[source, 0:16], self_sem)
        copy.start()
        copy.wait()

    def wait_for(part, sem):
        pltpu.make_async_copy(part, part, sem).wait()

    for h, rows in ((0, 24), (1, 16)):
        @pl.when(jnp.logical_and(half == h, selfish))
        def _():
            wait_for(landed.at[0:15, 0:rows], far_recv)

        @pl.when(jnp.logical_and(half == h, jnp.logical_not(selfish)))
        def _():
            wait_for(landed.at[:, 0:rows], far_recv)

    wait_for(own_ref.at[0:15], near_send)
    for flag, index, buffer in ((early_self, 0, early), (late_self, 1, late)):
        @pl.when(flag)
        def _():
            wait_for(buffer.at[0:7], far_send.at[index])

        @pl.when(jnp.logical_not(flag))
        def _():
            wait_for(buffer, far_send.at[index])


def finish_kernel(landed, out_ref, result, out_sem):
    chunk = iota((8, LANES), 1) // 8
    has_ninth = jnp.broadcast_to(lax.axis_index("tm"), (8, LANES)) == 0
    writes = []
    for xx in range(2):
        for pair in range(2):
            block = xx * 2 + pair
            tiles = []
            ninth = jnp.zeros((8, LANES), jnp.float32)
            for low in range(2):
                at = pair * 2 + low
                for zz in range(8):
                    tiles.append(landed[xx * 8 + zz, at * 4 : at * 4 + 8, :])
                    to = low * 8 + zz
                    ninth = jnp.where(
                        chunk == to, pltpu.roll(landed[xx * 8 + zz, 16:24, :], (to - at) * 8 % LANES, 1), ninth
                    )
            ninth = jnp.where(has_ninth, ninth, 0.0)
            tiles = swap_chunks(tiles)
            for high in range(2):
                for frame in range(8):
                    now = tiles[high * 8 + frame][0:4]
                    if frame < 7:
                        later = tiles[high * 8 + frame + 1][0:4]
                    else:
                        later = ninth[high * 4 : high * 4 + 4]
                    first = high * 64 + frame
                    result[block, pl.ds(first, 4, stride=16), :] = now * (1.0 / (FSUM * 8))
                    result[block, pl.ds(first + 8, 4, stride=16), :] = (now + later) * (1.0 / (FSUM * 16))
            write = pltpu.make_async_copy(
                result.at[block], out_ref.at[:, pl.ds(block * LANES, LANES)], out_sem.at[block]
            )
            write.start()
            writes.append(write)
    for write in writes:
        write.wait()


def finish(landed):
    return pl.pallas_call(
        finish_kernel,
        out_shape=pltpu.HBM((8 * BOXES * FRAMES, 512), jnp.float32),
        in_specs=[pl.BlockSpec(memory_space=pltpu.VMEM)],
        out_specs=pl.BlockSpec(memory_space=pltpu.HBM),
        scratch_shapes=[
            pltpu.VMEM((4, 128, LANES), jnp.float32),
            pltpu.SemaphoreType.DMA((4,)),
        ],
        compiler_params=pltpu.CompilerParams(vmem_limit_bytes=16 * 2**20),
        name="finish",
    )(landed)


def search(voltages, feed_slot, tree_shift):
    level = pltpu.VMEM((2, 8, 24, LANES), jnp.float32)
    dma = pltpu.SemaphoreType.DMA
    return pl.pallas_call(
        search_kernel,
        out_shape=pltpu.VMEM((16, 24, LANES), jnp.float32),
        in_specs=[pl.BlockSpec(memory_space=pltpu.HBM)] * 4,
        out_specs=pl.BlockSpec(memory_space=pltpu.VMEM),
        scratch_shapes=[
            pltpu.SMEM((FEEDS // LANES, LANES), jnp.int32),
            pltpu.VMEM((FEEDS // LANES, LANES), jnp.int32),
            pltpu.SMEM((FEEDS // LANES, LANES), jnp.int32),
            pltpu.SMEM((14,), jnp.int32),
            pltpu.VMEM((2 * SAMPLES, FEEDS), jnp.bfloat16),
            pltpu.VMEM((NS, NS), jnp.float32),
            pltpu.VMEM((FEEDS * 8, LANES), jnp.float32),
            [pltpu.VMEM((NS * 8, LANES), jnp.float32)] * (POL * EW),
            pltpu.VMEM((POL * EW, NS, 2 * SAMPLES), jnp.float32),
            pltpu.VMEM((EW, NS, SAMPLES), jnp.float32),
            pltpu.VMEM((EW, NS, SAMPLES), jnp.bfloat16),
            pltpu.VMEM((EW, NS, SAMPLES), jnp.bfloat16),
            pltpu.VMEM((MEMBERS, 16, LANES), jnp.float32),
            pltpu.VMEM((MEMBERS, 16, LANES), jnp.float32),
            level,
            level,
            level,
            pltpu.VMEM((2, 128, LANES), jnp.float32),
            pltpu.VMEM((8, 24, LANES), jnp.float32),
            pltpu.VMEM((8, 16, LANES), jnp.float32),
            dma,
            dma,
            dma,
            dma((SPLIT,)),
            dma,
            dma,
            dma,
            dma((2,)),
            dma,
            dma,
        ],
        compiler_params=pltpu.CompilerParams(
            collective_id=0, has_side_effects=True, vmem_limit_bytes=60 * 2**20
        ),
        name="search",
    )(
        feed_slot.reshape(FEEDS // LANES, LANES),
        tree_shift,
        voltages.reshape(2 * SAMPLES, FEEDS),
        steer_table(),
    )


def on_device(voltages, feed_slot, tree_shift):
    result = finish(search(voltages, feed_slot, tree_shift))
    return result.reshape(8, BOXES, FRAMES, 512)


def solution(mesh):
    placed = (P(None, "tm", "beam", None), P(), P())
    return jax.shard_map(
        on_device,
        mesh=mesh,
        in_specs=placed,
        out_specs=P("beam", None, "tm", None),
        check_vma=False,
    )
```
